256 devices in a mesh: dp: 16 (over y, x_lo, core), expert: 16 (over z, x_hi).
Axes of the slice: x: 4 (x_hi: 2, x_lo: 2; x = x_hi * 2 + x_lo), y: 4, z: 8, core: 2. Of those that a mesh axis runs over, the one named last changes fastest.
Arguments:
- tokens: bfloat16 [2048, 3584], P('expert', 'dp'), may hold values from -6 to 6
- grad_out: bfloat16 [2048, 3584], P('expert', 'dp'), may hold values from -6 to 6
- routing: int32 [2048, 8], P('expert'), may hold values from 0 to 31, all different within a row; in each aligned block of 128 rows (0 to 127, 128 to 255, ...) at most 40 rows name the same one
- gates: bfloat16 [2048, 8], P('expert'), may hold values from 0.029907227 to 0.59765625
- w_gate: bfloat16 [32, 3584, 2048], P('expert', None, 'dp'), may hold values from -0.09375 to 0.09375
- w_up: bfloat16 [32, 3584, 2048], P('expert', None, 'dp'), may hold values from -0.09375 to 0.09375
- w_down: bfloat16 [32, 2048, 3584], P('expert', 'dp'), may hold values from -0.125 to 0.125
Outputs:
- grad_tokens: bfloat16 [2048, 3584], P('expert', 'dp')
- grad_gates: float32 [2048, 8], P('expert')
- grad_w_gate: bfloat16 [32, 3584, 2048], P('expert', None, 'dp')
- grad_w_up: bfloat16 [32, 3584, 2048], P('expert', None, 'dp')
- grad_w_down: bfloat16 [32, 2048, 3584], P('expert', 'dp')
The draws below stay inside these ranges and needn't reach their ends.
Inputs may be any that keep to these rules, and one draw needn't show every extreme that they name: `routing`: each row names 8 different experts. Among the 128 rows of one index of expert no expert is named by more than 40 rows, and in some of them one expert is named by exactly 40 rows.
All inputs are finite; a program needn't handle non-finite values.
Results may differ from the reference program's by a relative error of at most 0.014.
Values may be sent and summed in bfloat16 or wider, within the bound.
No kernel may reach another device: no remote copies, remote signals or barrier semaphores. Data moves between devices by JAX's collectives and lax.ppermute only.
A program may use at most 192 MiB of HBM per device.

```python
import math
import jax
import jax.numpy as jnp
import numpy as np
from jax import lax

D = 3584
FF = 2048
TOPK = 8
TOK_DEV = 128
EXPERTS = 32
TOKENS = 2048
CAP = 40
N_DP = 16
N_EXPERT = 16


def levels(own_key, extent, pieces, smallest, high):
    def one(dim, shards_of):
        steps = jax.random.uniform(jax.random.fold_in(jax.random.fold_in(own_key, 6), dim), (shards_of,), jnp.float32, smallest / len(pieces), high / len(pieces))
        return jnp.repeat(jnp.exp(steps), extent[dim] // shards_of).reshape((-1,) + (1,) * (len(extent) - dim - 1))

    factor_of = one(*pieces[0])
    for cut in pieces[1:]:
        factor_of = factor_of * one(*cut)
    return factor_of


def assign_block(key, own, number, rows, amount, top, bound, lean):
    order = jax.random.permutation(key, amount)
    heavy_load, ordinary = portions_of(amount, rows * top, bound, lean, True), portions_of(amount, rows * top, bound, lean, False)
    places = jnp.arange(amount)

    def named(tallies, rotation):
        used = int((tallies > 0).sum())
        fixed = max(1, used // 4)
        passed = fixed + (places - fixed + rotation * (used - fixed)) % max(1, amount - fixed)
        return jnp.zeros((amount,), jnp.int32).at[order[jnp.where(places < fixed, places, passed)]].set(jnp.asarray(tallies, jnp.int32))

    tallies = jnp.where(number % 4 == 0, named(heavy_load, number // 4), named(ordinary, number - number // 4 - 1))
    mixed = jax.random.permutation(jax.random.fold_in(own, 3), amount)
    giver, taker = mixed[0:amount // 2 * 2:2], mixed[1:amount // 2 * 2:2]
    margin = jnp.minimum(tallies[giver] - 1, bound - tallies[taker]) // 2
    margin = jnp.where((giver == order[0]) | (taker == order[0]) | (tallies[taker] == 0), 0, jnp.maximum(margin, 0))
    passed = jax.random.randint(jax.random.fold_in(own, 4), (amount // 2,), 0, 1 << 20) % (margin + 1)
    tallies = tallies.at[giver].add(-passed).at[taker].add(passed)
    items = jnp.searchsorted(jnp.cumsum(tallies), jnp.arange(rows * top), side="right").astype(jnp.int32)
    listing = items.reshape(top, rows).T
    listing = listing[jax.random.permutation(jax.random.fold_in(own, 1), rows)]
    rotation = jax.random.randint(jax.random.fold_in(own, 2), (rows, 1), 0, top)
    return jnp.take_along_axis(listing, (jnp.arange(top)[None, :] + rotation) % top, axis=1)


def portions_of(number_of, total, limit, skew, full):
    portions = [(1 << 20) // math.isqrt(rank ** skew) + 1 for rank in range(1, number_of + 1)]
    largest = limit if full else min(limit, max(-(-total // number_of), total * portions[0] // sum(portions)))
    least = 1 if total - largest >= number_of - 1 else 0
    holding, spare = [largest] + [least] * (number_of - 1), total - largest - least * (number_of - 1)
    while spare > 0:
        candidates = [i for i in range(1, number_of) if holding[i] < largest] or [i for i in range(1, number_of) if holding[i] < limit]
        mass, left = sum([portions[i] for i in candidates]), spare
        for i in candidates:
            extra = min(limit - holding[i], max(1, left * portions[i] // mass), spare)
            holding[i] = holding[i] + extra
            spare = spare - extra
    return np.array(holding)


def centred(key, extent, spread, reach, pieces=(), kind=jnp.bfloat16):
    factor_of = levels(key, extent, pieces, -0.22, 0.18) if pieces else 1.0
    result = jax.random.normal(key, extent, jnp.float32) * spread * factor_of
    return jnp.minimum(jnp.maximum(result, -reach), reach).astype(kind)


def setup_inputs(seed: int = 0) -> dict:
    keys = jax.random.split(jax.random.key(seed), 8)
    tokens = centred(keys[0], (TOKENS, D), 1.0, 6.0, ((0, 16), (1, 16)))
    grad_out = centred(keys[1], (TOKENS, D), 1.0, 6.0, ((0, 16), (1, 16)))
    routing_keys = jax.random.split(jax.random.fold_in(keys[2], 1), TOKENS // TOK_DEV)
    routing_turns = jax.random.permutation(jax.random.fold_in(keys[2], 3), TOKENS // TOK_DEV)
    routing = jax.vmap(lambda own, number: assign_block(jax.random.fold_in(keys[2], 2), own, number, TOK_DEV, EXPERTS, TOPK, CAP, 2))(routing_keys, routing_turns).reshape((TOKENS, TOPK))
    gates = jnp.clip(jnp.exp(math.log(0.59765625) - 2.99491561 * jax.random.uniform(keys[3], (TOKENS, TOPK), jnp.float32) ** levels(keys[3], (TOKENS, TOPK), ((0, 16),), -0.2, 0.2)), 0.029907227, 0.59765625).astype(jnp.bfloat16)
    w_gate = centred(keys[4], (EXPERTS, D, FF), D ** -0.5, 0.09375, ((0, 16), (2, 16)))
    w_up = centred(keys[5], (EXPERTS, D, FF), D ** -0.5, 0.09375, ((0, 16), (2, 16)))
    w_down = centred(keys[6], (EXPERTS, FF, D), FF ** -0.5, 0.125, ((0, 16), (1, 16)))
    return {"tokens": tokens, "grad_out": grad_out, "routing": routing, "gates": gates, "w_gate": w_gate, "w_up": w_up, "w_down": w_down}


def slot_table(routing):
    onehot = (routing[:, :, None] == jnp.arange(EXPERTS, dtype=jnp.int32)[None, None, :]).astype(jnp.int32)
    per_token = jnp.sum(onehot, axis=1)
    blocks = per_token.reshape(N_EXPERT, TOK_DEV, EXPERTS)
    earlier = (jnp.cumsum(blocks, axis=1) - blocks).reshape(TOKENS, EXPERTS)
    position = jnp.sum(onehot * earlier[:, None, :], axis=2)
    source = jnp.arange(TOKENS, dtype=jnp.int32) // TOK_DEV
    return routing * (N_EXPERT * CAP) + source[:, None] * CAP + position


def reference(tokens, grad_out, routing, gates, w_gate, w_up, w_down):
    row_count = N_EXPERT * CAP
    group_width = FF // N_DP
    table_len = EXPERTS * row_count
    slot_ids = slot_table(routing).reshape(-1).astype(jnp.int32)
    token_ids = jnp.repeat(jnp.arange(TOKENS, dtype=jnp.int32), TOPK)
    pair_ids = jnp.arange(TOKENS * TOPK, dtype=jnp.int32)
    table_token = jnp.zeros((table_len,), jnp.int32).at[slot_ids].set(token_ids).reshape(EXPERTS, row_count)
    table_pair = jnp.zeros((table_len,), jnp.int32).at[slot_ids].set(pair_ids).reshape(EXPERTS, row_count)
    table_live = jnp.zeros((table_len,), jnp.float32).at[slot_ids].set(1.0).reshape(EXPERTS, row_count)
    table_gate = jnp.zeros((table_len,), jnp.float32).at[slot_ids].set(gates.reshape(-1).astype(jnp.float32)).reshape(EXPERTS, row_count)

    def expert_step(carry, inputs):
        token_acc, pair_acc = carry
        token_row, pair_row, live_slot, gate_value, weight_gate, weight_up, weight_down = inputs
        live_mask = live_slot.astype(jnp.bfloat16)[:, None]
        input_rows = tokens[token_row] * live_mask
        grad_rows = grad_out[token_row] * live_mask
        gate_pre = jnp.dot(input_rows, weight_gate, preferred_element_type=jnp.float32)
        up_pre = jnp.dot(input_rows, weight_up, preferred_element_type=jnp.float32)
        sigma = jax.nn.sigmoid(gate_pre)
        act = (gate_pre * sigma * up_pre).astype(jnp.bfloat16)
        raw = jnp.dot(grad_rows, weight_down.T, preferred_element_type=jnp.float32)
        group_part = jnp.sum((act.astype(jnp.float32) * raw).reshape(row_count, N_DP, group_width), axis=2)
        group_part = lax.optimization_barrier(group_part.astype(jnp.bfloat16))
        pair_grad = jnp.sum(group_part.astype(jnp.float32), axis=1)
        dact = gate_value[:, None] * raw
        grad_gate_pre = (dact * up_pre * sigma * (1.0 + gate_pre * (1.0 - sigma))).astype(jnp.bfloat16)
        grad_up_pre = (dact * gate_pre * sigma).astype(jnp.bfloat16)
        scaled_grad = (gate_value[:, None] * grad_rows.astype(jnp.float32)).astype(jnp.bfloat16)
        grad_wg = jnp.dot(input_rows.T, grad_gate_pre, preferred_element_type=jnp.float32).astype(jnp.bfloat16)
        grad_wu = jnp.dot(input_rows.T, grad_up_pre, preferred_element_type=jnp.float32).astype(jnp.bfloat16)
        grad_wd = jnp.dot(act.T, scaled_grad, preferred_element_type=jnp.float32).astype(jnp.bfloat16)
        term = jnp.einsum("rgf,dgf->rgd", grad_gate_pre.astype(jnp.float32).reshape(row_count, N_DP, group_width),
                          weight_gate.astype(jnp.float32).reshape(D, N_DP, group_width))
        term = term + jnp.einsum("rgf,dgf->rgd", grad_up_pre.astype(jnp.float32).reshape(row_count, N_DP, group_width),
                                 weight_up.astype(jnp.float32).reshape(D, N_DP, group_width))
        term = lax.optimization_barrier(term.astype(jnp.bfloat16))
        token_term = jnp.sum(term.astype(jnp.float32), axis=1) * live_slot[:, None]
        token_acc = token_acc.at[token_row].add(token_term)
        pair_acc = pair_acc.at[pair_row].add(pair_grad * live_slot)
        return (token_acc, pair_acc), (grad_wg, grad_wu, grad_wd)

    start = (jnp.zeros((TOKENS, D), jnp.float32), jnp.zeros((TOKENS * TOPK,), jnp.float32))
    (token_acc, pair_acc), (grad_w_gate, grad_w_up, grad_w_down) = lax.scan(
        expert_step, start, (table_token, table_pair, table_live, table_gate, w_gate, w_up, w_down))
    return (token_acc.astype(jnp.bfloat16), pair_acc.reshape(TOKENS, TOPK), grad_w_gate, grad_w_up, grad_w_down)
```

```python
import jax
import jax.numpy as jnp
from jax import lax
from jax.sharding import Mesh, PartitionSpec as P

BF = jnp.bfloat16
F32 = jnp.float32
DP = ("y", "xl", "core")
EX = ("z", "xh")


def shift(x, axis, by):
    n = lax.axis_size(axis)
    return lax.ppermute(x, axis, [(i, (i + by) % n) for i in range(n)])


def dot(a, b, ca, cb):
    return lax.dot_general(a, b, (((ca,), (cb,)), ((), ())), preferred_element_type=F32)


def total(x, axis):
    n = lax.axis_size(axis)
    step = 1
    while step < n:
        x = x + lax.ppermute(x, axis, [(i, i ^ step) for i in range(n)])
        step *= 2
    return x


def per_device(tokens, grad_out, routing, gates, w_gate, w_up, w_down):
    toks, topk = routing.shape
    peers = lax.axis_size("z") * lax.axis_size("xh")
    experts = peers * w_gate.shape[0]
    cap = min(toks, 5 * toks * topk // (4 * experts))
    half = w_gate.shape[2]
    core = lax.axis_index("core")
    yi = lax.axis_index("y")
    ny = lax.axis_size("y")
    rows = peers * cap

    def pick(w):
        own = lax.dynamic_index_in_dim(w, core, 0, keepdims=False)
        give = lax.dynamic_index_in_dim(w, 1 - core, 0, keepdims=False)
        return own, shift(give, "core", 1)

    gate_own, gate_oth = pick(w_gate)
    up_own, up_oth = pick(w_up)
    down_own, down_oth = pick(w_down)

    both = jnp.concatenate([tokens, grad_out], axis=0)
    both = lax.all_gather(both, ("xl", "core"), axis=1, tiled=True)
    tok4, grad4 = both[:toks], both[toks:]
    width = tok4.shape[1]

    route_t = routing.T
    gates_t = gates.T.astype(F32)
    ids = 2 * jnp.arange(peers, dtype=jnp.int32) + core
    hit = route_t[None, :, :] == ids[:, None, None]
    chosen = jnp.any(hit, axis=1)
    gate_of = jnp.sum(jnp.where(hit, gates_t[None], 0.0), axis=1)
    upper = jnp.triu(jnp.ones((toks, toks), BF), 1)
    earlier = dot(chosen.astype(BF), upper, 1, 0).astype(jnp.int32)
    match = chosen[:, None, :] & (
        earlier[:, None, :] == jnp.arange(cap, dtype=jnp.int32)[None, :, None]
    )
    placing = match.astype(BF).reshape(rows, toks)
    weighted = jnp.where(match, gate_of[:, None, :], 0.0).astype(BF).reshape(rows, toks)

    def out_rows(place, x):
        sent = dot(place, x, 1, 0).astype(BF).reshape(peers, cap, width)
        got = lax.all_to_all(sent, EX, 0, 0, tiled=True)
        return got.reshape(rows, width)

    def ring(x):
        prev = shift(x, "y", 1)
        nxt = shift(x, "y", -1)
        h = rows // 2
        far = jnp.concatenate([shift(prev[:h], "y", 1), shift(nxt[h:], "y", -1)], axis=0)
        return [x, nxt, far, prev]

    xs = ring(out_rows(placing, tok4))
    gs = ring(out_rows(weighted, grad4))

    wcat = jnp.concatenate([gate_own, up_own, gate_oth, up_oth], axis=1).reshape(
        ny, width, 4 * half
    )
    wdown = jnp.concatenate([down_own, down_oth], axis=0)
    wj = [
        lax.dynamic_index_in_dim(wcat, (yi + j) % ny, 0, keepdims=False) for j in range(ny)
    ]
    dj = [
        lax.dynamic_slice_in_dim(wdown, ((yi + j) % ny) * width, width, 1) for j in range(ny)
    ]

    def added(parts):
        s = parts[0]
        for p in parts[1:]:
            s = s + p
        return s

    order = [0, 1, 3, 2]
    pre = added([dot(xs[j], wj[j], 1, 0) for j in order])
    dact = added([dot(gs[j], dj[j], 1, 1) for j in order])

    def cells(gate_pre, up_pre, da):
        sig = jax.nn.sigmoid(gate_pre)
        act = (gate_pre * sig * up_pre).astype(BF)
        pair = jnp.sum(act.astype(F32) * da, axis=1)
        gg = (da * up_pre * sig * (1.0 + gate_pre * (1.0 - sig))).astype(BF)
        gu = (da * gate_pre * sig).astype(BF)
        return act, pair, gg, gu

    a0, p0, gg0, gu0 = cells(pre[:, :half], pre[:, half : 2 * half], dact[:, :half])
    a1, p1, gg1, gu1 = cells(
        pre[:, 2 * half : 3 * half], pre[:, 3 * half :], dact[:, half:]
    )
    grads = jnp.concatenate([gg0, gu0, gg1, gu1], axis=1)
    act = jnp.concatenate([a0, a1], axis=1)

    h = rows // 2
    t_far = dot(grads, wj[2], 1, 1).astype(BF)
    from_prev = shift(t_far[:h], "y", 1)
    from_next = shift(t_far[h:], "y", -1)
    t_next = dot(grads, wj[1], 1, 1)
    t_prev = dot(grads, wj[3], 1, 1)
    zero = jnp.zeros((h, width), F32)
    t_next = (t_next + jnp.concatenate([from_prev.astype(F32), zero], axis=0)).astype(BF)
    t_prev = (t_prev + jnp.concatenate([zero, from_next.astype(F32)], axis=0)).astype(BF)
    got_a = shift(t_next, "y", 1)
    got_b = shift(t_prev, "y", -1)
    t_own = dot(grads, wj[0], 1, 1) + got_a.astype(F32) + got_b.astype(F32)
    back = lax.all_to_all(
        t_own.astype(BF).reshape(peers, cap, width), EX, 0, 0, tiled=True
    ).reshape(rows, width)

    pair_back = lax.all_to_all((p0 + p1).reshape(peers, cap), EX, 0, 0, tiled=True)
    of_token = jnp.sum(jnp.where(match, pair_back[:, :, None], 0.0), axis=1)
    pair_sum = jnp.sum(jnp.where(hit, of_token[:, None, :], 0.0), axis=0)
    for axis in ("core", "xl", "y"):
        pair_sum = total(pair_sum, axis)
    grad_gates = (pair_sum / gates_t).T

    part = dot(placing, back, 0, 0)
    piece = tokens.shape[1]
    xl = lax.axis_index("xl")
    quarters = [part[:, i * piece : (i + 1) * piece] for i in range(4)]
    x_own = jnp.where(xl == 0, part[:, : 2 * piece], part[:, 2 * piece :])
    x_give = jnp.where(xl == 0, part[:, 2 * piece :], part[:, : 2 * piece])
    x_sum = x_own + shift(x_give, "xl", 1)
    c_own = jnp.where(core == 0, x_sum[:, :piece], x_sum[:, piece:])
    c_give = jnp.where(core == 0, x_sum[:, piece:], x_sum[:, :piece])
    grad_tokens = (c_own + shift(c_give, "core", 1)).astype(BF)

    gw = jnp.zeros((ny, width, 4 * half), BF)
    gd = jnp.zeros((2 * half, ny * width), BF)
    for j in range(ny):
        at = (yi + j) % ny
        gw = lax.dynamic_update_index_in_dim(gw, dot(xs[j], grads, 0, 0).astype(BF), at, 0)
        gd = lax.dynamic_update_slice_in_dim(
            gd, dot(act, gs[j], 0, 0).astype(BF), at * width, 1
        )
    gw = gw.reshape(ny * width, 4 * half)

    def paired(own, give):
        got = shift(give, "core", 1)
        return jnp.stack([jnp.where(core == 0, own, got), jnp.where(core == 0, got, own)])

    grad_gate = paired(gw[:, :half], gw[:, 2 * half : 3 * half])
    grad_up = paired(gw[:, half : 2 * half], gw[:, 3 * half :])
    grad_down = paired(gd[:half], gd[half:])
    return grad_tokens, grad_gates, grad_gate, grad_up, grad_down


def solution(mesh):
    fine = Mesh(mesh.devices.reshape(4, 2, 2, 8, 2), DP + EX)
    return jax.shard_map(
        per_device,
        mesh=fine,
        in_specs=(
            P(EX, DP),
            P(EX, DP),
            P(EX, None),
            P(EX, None),
            P(EX, None, DP),
            P(EX, None, DP),
            P(EX, DP, None),
        ),
        out_specs=(
            P(EX, DP),
            P(EX, None),
            P(EX, None, DP),
            P(EX, None, DP),
            P(EX, DP, None),
        ),
        check_vma=False,
    )
```

```python
import jax
import jax.numpy as jnp
from jax import lax
from jax.sharding import Mesh, PartitionSpec as P

BF = jnp.bfloat16
F32 = jnp.float32
DP = ("y", "xl", "core")
EX = ("z", "xh")
STEPS = ((0, 1, 7, 2), (6, 3, 5, 4))


def shift(x, axis, by):
    n = lax.axis_size(axis)
    return lax.ppermute(x, axis, [(i, (i + by) % n) for i in range(n)])


def send(x, step, back=False):
    pairs = []
    for xl in range(2):
        for z in range(8):
            for xh in range(2):
                here = (xl * 8 + z) * 2 + xh
                there = (xl * 8 + (z + step) % 8) * 2 + (xh + xl) % 2
                pairs.append((there, here) if back else (here, there))
    return lax.ppermute(x, ("xl", "z", "xh"), pairs)


def dot(a, b, ca, cb):
    return lax.dot_general(a, b, (((ca,), (cb,)), ((), ())), preferred_element_type=F32)


def total(x, axis):
    n = lax.axis_size(axis)
    step = 1
    while step < n:
        x = x + lax.ppermute(x, axis, [(i, i ^ step) for i in range(n)])
        step *= 2
    return x


def after(x, *others):
    return lax.optimization_barrier((x,) + others)[0]


def per_device(tokens, grad_out, routing, gates, w_gate, w_up, w_down):
    toks, topk = routing.shape
    peers = lax.axis_size("z") * lax.axis_size("xh")
    experts = peers * w_gate.shape[0]
    cap = min(toks, 5 * toks * topk // (4 * experts))
    half = w_gate.shape[2]
    core = lax.axis_index("core")
    yi = lax.axis_index("y")
    zi = lax.axis_index("z")
    xl = lax.axis_index("xl")
    xh = lax.axis_index("xh")
    ny = lax.axis_size("y")
    steps = STEPS[0] + STEPS[1]
    per = len(STEPS[0]) * cap

    def pick(w):
        own = lax.dynamic_index_in_dim(w, core, 0, keepdims=False)
        give = lax.dynamic_index_in_dim(w, 1 - core, 0, keepdims=False)
        return own, shift(give, "core", 1)

    both = jnp.concatenate([tokens, grad_out], axis=0)
    both = lax.all_gather(both, ("xl", "core"), axis=1, tiled=True)
    tok4, grad4 = both[:toks], both[toks:]
    width = tok4.shape[1]

    route_t = routing.T
    gates_t = gates.T.astype(F32)
    dest = ((zi + jnp.array(steps, jnp.int32)) % 8) * 2 + (xh + xl) % 2
    ids = 2 * dest + core
    hit = route_t[None, :, :] == ids[:, None, None]
    chosen = jnp.any(hit, axis=1)
    gate_of = jnp.sum(jnp.where(hit, gates_t[None], 0.0), axis=1)
    upper = jnp.triu(jnp.ones((toks, toks), BF), 1)
    earlier = dot(chosen.astype(BF), upper, 1, 0).astype(jnp.int32)
    match = chosen[:, None, :] & (
        earlier[:, None, :] == jnp.arange(cap, dtype=jnp.int32)[None, :, None]
    )
    rows = len(steps) * cap
    placing = match.astype(BF).reshape(rows, toks)
    weighted = jnp.where(match, gate_of[:, None, :], 0.0).astype(BF).reshape(rows, toks)

    def blocks(sent, c):
        base = c * len(STEPS[0])
        return jnp.concatenate(
            [send(sent[(base + k) * cap : (base + k + 1) * cap], s) for k, s in enumerate(STEPS[c])],
            axis=0,
        )

    def ring(own):
        x = jnp.concatenate([own, shift(own, "xl", 1)], axis=0)
        prev = shift(x, "y", 1)
        nxt = shift(x, "y", -1)
        far = jnp.concatenate(
            [shift(prev[:per], "y", 1), shift(nxt[per:], "y", -1)], axis=0
        )
        return [x, nxt, far, prev]

    tsent = dot(placing, tok4, 1, 0).astype(BF)
    t_got = [blocks(tsent, 0), blocks(tsent, 1)]
    gsent = dot(weighted, grad4, 1, 0).astype(BF)
    gsent = after(gsent, t_got[0])
    g_got = [blocks(gsent, 0)]
    g_got.append(blocks(after(gsent, t_got[1]), 1))
    xs = [ring(t) for t in t_got]
    gs = [ring(t) for t in g_got]

    gate_own, gate_oth = pick(w_gate)
    up_own, up_oth = pick(w_up)
    down_own, down_oth = pick(w_down)
    wcat = jnp.concatenate([gate_own, up_own, gate_oth, up_oth], axis=1).reshape(
        ny, width, 4 * half
    )
    wdown = jnp.concatenate([down_own, down_oth], axis=0)
    wj = [
        lax.dynamic_index_in_dim(wcat, (yi + j) % ny, 0, keepdims=False) for j in range(ny)
    ]
    dj = [
        lax.dynamic_slice_in_dim(wdown, ((yi + j) % ny) * width, width, 1) for j in range(ny)
    ]

    def added(parts):
        s = parts[0]
        for p in parts[1:]:
            s = s + p
        return s

    order = [0, 1, 3, 2]

    def cells(gate_pre, up_pre, da):
        sig = jax.nn.sigmoid(gate_pre)
        act = (gate_pre * sig * up_pre).astype(BF)
        pair = jnp.sum(act.astype(F32) * da, axis=1)
        gg = (da * up_pre * sig * (1.0 + gate_pre * (1.0 - sig))).astype(BF)
        gu = (da * gate_pre * sig).astype(BF)
        return act, pair, gg, gu

    grads, acts, pairs, backs = [], [], [], []
    for c in range(2):
        pre = added([dot(xs[c][j], wj[j], 1, 0) for j in order])
        dact = added([dot(gs[c][j], dj[j], 1, 1) for j in order])
        a0, p0, gg0, gu0 = cells(pre[:, :half], pre[:, half : 2 * half], dact[:, :half])
        a1, p1, gg1, gu1 = cells(
            pre[:, 2 * half : 3 * half], pre[:, 3 * half :], dact[:, half:]
        )
        g = jnp.concatenate([gg0, gu0, gg1, gu1], axis=1)
        grads.append(g)
        acts.append(jnp.concatenate([a0, a1], axis=1))
        pairs.append(p0 + p1)

        t_far = dot(g, wj[2], 1, 1).astype(BF)
        from_prev = shift(t_far[:per], "y", 1)
        from_next = shift(t_far[per:], "y", -1)
        t_next = dot(g, wj[1], 1, 1)
        t_prev = dot(g, wj[3], 1, 1)
        zero = jnp.zeros((per, width), F32)
        t_next = (t_next + jnp.concatenate([from_prev.astype(F32), zero], axis=0)).astype(BF)
        t_prev = (t_prev + jnp.concatenate([zero, from_next.astype(F32)], axis=0)).astype(BF)
        got_a = shift(t_next, "y", 1)
        got_b = shift(t_prev, "y", -1)
        t_own = dot(g, wj[0], 1, 1) + got_a.astype(F32) + got_b.astype(F32)
        give = shift(t_own[per:].astype(BF), "xl", 1)
        mine = (t_own[:per] + give.astype(F32)).astype(BF)
        for k, s in enumerate(STEPS[c]):
            backs.append(send(mine[k * cap : (k + 1) * cap], s, back=True))

    pair_x = jnp.concatenate(
        [p[:per] + shift(p[per:], "xl", 1) for p in pairs], axis=0
    ).reshape(len(steps), 1, cap)
    pair_back = jnp.concatenate(
        [send(pair_x[k], s, back=True) for k, s in enumerate(steps)], axis=0
    )
    of_token = jnp.sum(jnp.where(match, pair_back[:, :, None], 0.0), axis=1)
    pair_sum = jnp.sum(jnp.where(hit, of_token[:, None, :], 0.0), axis=0)
    for axis in ("core", "xl", "y"):
        pair_sum = total(pair_sum, axis)
    grad_gates = (pair_sum / gates_t).T

    part = dot(placing, jnp.concatenate(backs, axis=0), 0, 0)
    piece = tokens.shape[1]
    x_own = jnp.where(xl == 0, part[:, : 2 * piece], part[:, 2 * piece :])
    x_give = jnp.where(xl == 0, part[:, 2 * piece :], part[:, : 2 * piece])
    x_sum = x_own + shift(x_give, "xl", 1)
    c_own = jnp.where(core == 0, x_sum[:, :piece], x_sum[:, piece:])
    c_give = jnp.where(core == 0, x_sum[:, piece:], x_sum[:, :piece])
    grad_tokens = (c_own + shift(c_give, "core", 1)).astype(BF)

    gw = jnp.zeros((ny, width, 4 * half), BF)
    gd = jnp.zeros((2 * half, ny * width), BF)
    for j in range(ny):
        at = (yi + j) % ny
        piece_w = added([dot(xs[c][j], grads[c], 0, 0) for c in range(2)]).astype(BF)
        piece_d = added([dot(acts[c], gs[c][j], 0, 0) for c in range(2)]).astype(BF)
        gw = lax.dynamic_update_index_in_dim(gw, piece_w, at, 0)
        gd = lax.dynamic_update_slice_in_dim(gd, piece_d, at * width, 1)
    gw = gw.reshape(ny * width, 4 * half)

    def paired(own, give):
        got = shift(give, "core", 1)
        return jnp.stack([jnp.where(core == 0, own, got), jnp.where(core == 0, got, own)])

    grad_gate = paired(gw[:, :half], gw[:, 2 * half : 3 * half])
    grad_up = paired(gw[:, half : 2 * half], gw[:, 3 * half :])
    grad_down = paired(gd[:half], gd[half:])
    return grad_tokens, grad_gates, grad_gate, grad_up, grad_down


def solution(mesh):
    fine = Mesh(mesh.devices.reshape(4, 2, 2, 8, 2), DP + EX)
    return jax.shard_map(
        per_device,
        mesh=fine,
        in_specs=(
            P(EX, DP),
            P(EX, DP),
            P(EX, None),
            P(EX, None),
            P(EX, None, DP),
            P(EX, None, DP),
            P(EX, DP, None),
        ),
        out_specs=(
            P(EX, DP),
            P(EX, None),
            P(EX, None, DP),
            P(EX, None, DP),
            P(EX, DP, None),
        ),
        check_vma=False,
    )
```

```python
import jax
import jax.numpy as jnp
from jax import lax
from jax.sharding import Mesh, PartitionSpec as P

BF = jnp.bfloat16
F32 = jnp.float32
DP = ("y", "xl", "core")
EX = ("z", "xh")


def shift(x, axis, by):
    n = lax.axis_size(axis)
    return lax.ppermute(x, axis, [(i, (i + by) % n) for i in range(n)])


def dot(a, b, ca, cb):
    return lax.dot_general(a, b, (((ca,), (cb,)), ((), ())), preferred_element_type=F32)


def total(x, axis):
    n = lax.axis_size(axis)
    step = 1
    while step < n:
        x = x + lax.ppermute(x, axis, [(i, i ^ step) for i in range(n)])
        step *= 2
    return x


def after(x, *others):
    return lax.optimization_barrier((x,) + others)[0]


def per_device(tokens, grad_out, routing, gates, w_gate, w_up, w_down):
    toks, topk = routing.shape
    peers = lax.axis_size("z") * lax.axis_size("xh")
    experts = peers * w_gate.shape[0]
    cap = min(toks, 5 * toks * topk // (4 * experts))
    half = w_gate.shape[2]
    piece = tokens.shape[1]
    core = lax.axis_index("core")
    xl = lax.axis_index("xl")
    yi = lax.axis_index("y")
    ny = lax.axis_size("y")
    rows = peers * cap
    h = rows // 2

    both = jnp.concatenate([tokens, grad_out], axis=0)
    both = lax.all_gather(both, ("xl", "core"), axis=1, tiled=True)
    width = both.shape[1]
    mine = lax.dynamic_slice_in_dim(both, core * toks, toks, 0)

    route_t = routing.T
    gates_t = gates.T.astype(F32)
    ids = 2 * jnp.arange(peers, dtype=jnp.int32) + xl
    hit = route_t[None, :, :] == ids[:, None, None]
    chosen = jnp.any(hit, axis=1)
    gate_of = jnp.sum(jnp.where(hit, gates_t[None], 0.0), axis=1)
    upper = jnp.triu(jnp.ones((toks, toks), BF), 1)
    earlier = dot(chosen.astype(BF), upper, 1, 0).astype(jnp.int32)
    match = chosen[:, None, :] & (
        earlier[:, None, :] == jnp.arange(cap, dtype=jnp.int32)[None, :, None]
    )
    placing = match.astype(BF).reshape(rows, toks)
    scale = jnp.where(core == 0, 1.0, gate_of)
    weighted = jnp.where(match, scale[:, None, :], 0.0).astype(BF).reshape(rows, toks)

    sent = dot(weighted, mine, 1, 0).astype(BF).reshape(peers, cap, width)

    def pick(w):
        own = lax.dynamic_index_in_dim(w, xl, 0, keepdims=False)
        give = lax.dynamic_index_in_dim(w, 1 - xl, 0, keepdims=False)
        return own, shift(after(give, both), "xl", 1)

    gate_own, gate_oth = pick(w_gate)
    up_own, up_oth = pick(w_up)
    down_own, down_oth = pick(w_down)

    m0 = lax.all_to_all(sent, EX, 0, 0, tiled=True).reshape(rows, width)
    prev = shift(m0, "y", 1)
    nxt = shift(m0, "y", -1)
    far = [shift(prev[:h], "y", 1), shift(nxt[h:], "y", -1)]

    def swapped(m):
        o = shift(m, "core", 1)
        return jnp.where(core == 0, m, o), jnp.where(core == 0, o, m)

    x0, s0 = swapped(m0)
    xp, sp = swapped(prev)
    xn, sn = swapped(nxt)
    xf, sf = swapped(jnp.concatenate(far, axis=0))
    xs = [x0, xn, xf, xp]
    gs = [s0, sn, sf, sp]

    wcat = jnp.concatenate([gate_own, up_own, gate_oth, up_oth], axis=1).reshape(
        ny, width, 4 * half
    )
    wdown = jnp.concatenate([down_own, down_oth], axis=0)
    wj = [
        lax.dynamic_index_in_dim(wcat, (yi + j) % ny, 0, keepdims=False) for j in range(ny)
    ]
    dj = [
        lax.dynamic_slice_in_dim(wdown, ((yi + j) % ny) * width, width, 1) for j in range(ny)
    ]
    wparts = [w.reshape(2, 2, piece, 4 * half) for w in wj]
    keep = [
        lax.dynamic_index_in_dim(w, core, 1, keepdims=False).reshape(2 * piece, 4 * half)
        for w in wparts
    ]
    give = [
        lax.dynamic_index_in_dim(w, 1 - core, 1, keepdims=False).reshape(2 * piece, 4 * half)
        for w in wparts
    ]

    def added(parts):
        s = parts[0]
        for p in parts[1:]:
            s = s + p
        return s

    order = [0, 1, 3, 2]
    pre = added([dot(xs[j], wj[j], 1, 0) for j in order])
    dact = added([dot(gs[j], dj[j], 1, 1) for j in order])

    def cells(gate_pre, up_pre, da):
        sig = jax.nn.sigmoid(gate_pre)
        act = (gate_pre * sig * up_pre).astype(BF)
        pair = jnp.sum(act.astype(F32) * da, axis=1, keepdims=True)
        gg = (da * up_pre * sig * (1.0 + gate_pre * (1.0 - sig))).astype(BF)
        gu = (da * gate_pre * sig).astype(BF)
        return act, pair, gg, gu

    a0, p0, gg0, gu0 = cells(pre[:, :half], pre[:, half : 2 * half], dact[:, :half])
    a1, p1, gg1, gu1 = cells(
        pre[:, 2 * half : 3 * half], pre[:, 3 * half :], dact[:, half:]
    )
    grads = jnp.concatenate([gg0, gu0, gg1, gu1], axis=1)

    got = {}
    for j in (2, 1, 3, 0):
        got[j] = shift(dot(grads, give[j], 1, 1).astype(BF), "core", 1).astype(F32)
    t_far = (dot(grads, keep[2], 1, 1) + got[2]).astype(BF)
    from_prev = shift(t_far[:h], "y", 1)
    from_next = shift(t_far[h:], "y", -1)
    zero = jnp.zeros((h, 2 * piece), F32)
    t_next = dot(grads, keep[1], 1, 1) + got[1]
    t_prev = dot(grads, keep[3], 1, 1) + got[3]
    t_next = (t_next + jnp.concatenate([from_prev.astype(F32), zero], axis=0)).astype(BF)
    t_prev = (t_prev + jnp.concatenate([zero, from_next.astype(F32)], axis=0)).astype(BF)
    got_a = shift(t_next, "y", 1)
    got_b = shift(t_prev, "y", -1)
    t_own = dot(grads, keep[0], 1, 1) + got[0] + got_a.astype(F32) + got_b.astype(F32)

    pair = (p0 + p1).reshape(rows // 128, 128)
    pair = after(pair, from_prev)
    for axis in ("core", "y"):
        pair = total(pair, axis)
    pair = pair.reshape(rows, 1)
    pair_hi = pair.astype(BF)
    pair_lo = (pair - pair_hi.astype(F32)).astype(BF)
    lanes = 512 - 2 * piece
    full = jnp.concatenate(
        [t_own.astype(BF), pair_hi, pair_lo, jnp.zeros((rows, lanes - 2), BF)], axis=1
    )
    back = lax.all_to_all(
        full.reshape(peers, cap, 512), EX, 0, 0, tiled=True
    ).reshape(rows, 512)

    part = dot(placing, back[:, : 2 * piece], 0, 0)
    x_own = jnp.where(xl == 0, part[:, :piece], part[:, piece:])
    x_give = jnp.where(xl == 0, part[:, piece:], part[:, :piece])
    grad_tokens = (x_own + shift(x_give, "xl", 1)).astype(BF)

    pair_back = back[:, 2 * piece : 2 * piece + 1].astype(F32) + back[
        :, 2 * piece + 1 : 2 * piece + 2
    ].astype(F32)
    of_token = jnp.sum(jnp.where(match, pair_back.reshape(peers, cap, 1), 0.0), axis=1)
    pair_sum = jnp.sum(jnp.where(hit, of_token[:, None, :], 0.0), axis=0)
    pair_sum = total(pair_sum, "xl")
    grad_gates = (pair_sum / gates_t).T

    g_own = jnp.concatenate([gg0, gu0], axis=1)
    g_oth = jnp.concatenate([gg1, gu1], axis=1)

    def wide(g):
        out = jnp.zeros((ny, width, 2 * half), BF)
        for j in range(ny):
            out = lax.dynamic_update_index_in_dim(
                out, dot(xs[j], g, 0, 0).astype(BF), (yi + j) % ny, 0
            )
        return out.reshape(ny * width, 2 * half)

    def down(a):
        out = jnp.zeros((half, ny * width), BF)
        for j in range(ny):
            out = lax.dynamic_update_slice_in_dim(
                out, dot(a, gs[j], 0, 0).astype(BF), ((yi + j) % ny) * width, 1
            )
        return out

    w_got = shift(wide(g_oth), "xl", 1)
    d_got = shift(down(a1), "xl", 1)
    w_own = wide(g_own)
    d_own = down(a0)

    def paired(own, got):
        return jnp.stack([jnp.where(xl == 0, own, got), jnp.where(xl == 0, got, own)])

    grad_gate = paired(w_own[:, :half], w_got[:, :half])
    grad_up = paired(w_own[:, half:], w_got[:, half:])
    grad_down = paired(d_own, d_got)
    return grad_tokens, grad_gates, grad_gate, grad_up, grad_down


def solution(mesh):
    fine = Mesh(mesh.devices.reshape(4, 2, 2, 8, 2), DP + EX)
    return jax.shard_map(
        per_device,
        mesh=fine,
        in_specs=(
            P(EX, DP),
            P(EX, DP),
            P(EX, None),
            P(EX, None),
            P(EX, None, DP),
            P(EX, None, DP),
            P(EX, DP, None),
        ),
        out_specs=(
            P(EX, DP),
            P(EX, None),
            P(EX, None, DP),
            P(EX, None, DP),
            P(EX, DP, None),
        ),
        check_vma=False,
    )
```

```python
import jax
import jax.numpy as jnp
from jax import lax
from jax.sharding import Mesh, PartitionSpec as P

BF = jnp.bfloat16
F32 = jnp.float32
DP = ("y", "xl", "core")
EX = ("z", "xh")


def shift(x, axis, by):
    n = lax.axis_size(axis)
    return lax.ppermute(x, axis, [(i, (i + by) % n) for i in range(n)])


def dot(a, b, ca, cb):
    return lax.dot_general(a, b, (((ca,), (cb,)), ((), ())), preferred_element_type=F32)


def total(x, axis):
    n = lax.axis_size(axis)
    step = 1
    while step < n:
        x = x + lax.ppermute(x, axis, [(i, i ^ step) for i in range(n)])
        step *= 2
    return x


def after(x, *others):
    return lax.optimization_barrier((x,) + others)[0]


def per_device(tokens, grad_out, routing, gates, w_gate, w_up, w_down):
    toks, topk = routing.shape
    peers = lax.axis_size("z") * lax.axis_size("xh")
    experts = peers * w_gate.shape[0]
    cap = min(toks, 5 * toks * topk // (4 * experts))
    half = w_gate.shape[2]
    piece = tokens.shape[1]
    core = lax.axis_index("core")
    xl = lax.axis_index("xl")
    yi = lax.axis_index("y")
    ny = lax.axis_size("y")
    rows = peers * cap
    h = rows // 2

    both = jnp.concatenate([tokens, grad_out], axis=0)
    both = lax.all_gather(both, ("xl", "core"), axis=1, tiled=True)
    width = both.shape[1]
    mine = lax.dynamic_slice_in_dim(both, core * toks, toks, 0)

    route_t = routing.T
    gates_t = gates.T.astype(F32)
    ids = 2 * jnp.arange(peers, dtype=jnp.int32) + xl
    hit = route_t[None, :, :] == ids[:, None, None]
    chosen = jnp.any(hit, axis=1)
    gate_of = jnp.sum(jnp.where(hit, gates_t[None], 0.0), axis=1)
    upper = jnp.triu(jnp.ones((toks, toks), BF), 1)
    earlier = dot(chosen.astype(BF), upper, 1, 0).astype(jnp.int32)
    match = chosen[:, None, :] & (
        earlier[:, None, :] == jnp.arange(cap, dtype=jnp.int32)[None, :, None]
    )
    placing = match.astype(BF).reshape(rows, toks)
    scale = jnp.where(core == 0, 1.0, gate_of)
    weighted = jnp.where(match, scale[:, None, :], 0.0).astype(BF).reshape(rows, toks)

    sent = dot(weighted, mine, 1, 0).astype(BF).reshape(peers, cap, width)

    def pick(w, which):
        return lax.dynamic_index_in_dim(w, which, 0, keepdims=False)

    wide_own = jnp.concatenate([pick(w_gate, xl), pick(w_up, xl)], axis=1)
    wide_oth = jnp.concatenate([pick(w_gate, 1 - xl), pick(w_up, 1 - xl)], axis=1)
    wide_oth = shift(after(wide_oth, both), "xl", 1)
    down_own = pick(w_down, xl)
    down_oth = shift(after(pick(w_down, 1 - xl), both), "xl", 1)

    m0 = lax.all_to_all(sent, EX, 0, 0, tiled=True).reshape(rows, width)
    prev = shift(m0, "y", 1)
    nxt = shift(m0, "y", -1)
    far = [shift(prev[:h], "y", 1), shift(nxt[h:], "y", -1)]

    def swapped(m):
        o = shift(m, "core", 1)
        return jnp.where(core == 0, m, o), jnp.where(core == 0, o, m)

    x0, s0 = swapped(m0)
    xp, sp = swapped(prev)
    xn, sn = swapped(nxt)
    xf, sf = swapped(jnp.concatenate(far, axis=0))
    xs = [x0, xn, xf, xp]
    gs = [s0, sn, sf, sp]

    wcat = jnp.concatenate([wide_own, wide_oth], axis=1).reshape(ny, width, 4 * half)
    wdown = jnp.concatenate([down_own, down_oth], axis=0)
    wj = [
        lax.dynamic_index_in_dim(wcat, (yi + j) % ny, 0, keepdims=False) for j in range(ny)
    ]
    dj = [
        lax.dynamic_slice_in_dim(wdown, ((yi + j) % ny) * width, width, 1) for j in range(ny)
    ]
    wparts = [w.reshape(2, 2, piece, 4 * half) for w in wj]
    lanes = -(-(2 * piece + 1) // 128) * 128
    row = lax.broadcasted_iota(jnp.int32, (lanes, 128), 0)
    col = lax.broadcasted_iota(jnp.int32, (lanes, 128), 1)
    extra = ((row == 2 * piece) & (col < 2)).astype(BF)

    def halved(w, which):
        w = lax.dynamic_index_in_dim(w, which, 1, keepdims=False).reshape(2 * piece, 4 * half)
        w = jnp.pad(w, ((0, lanes - 2 * piece), (0, 0)))
        return jnp.concatenate([w, extra], axis=1)

    keep = [halved(w, core) for w in wparts]
    give = [halved(w, 1 - core) for w in wparts]

    def added(parts):
        s = parts[0]
        for p in parts[1:]:
            s = s + p
        return s

    order = [0, 1, 3, 2]
    pre = added([dot(xs[j], wj[j], 1, 0) for j in order])
    dact = added([dot(gs[j], dj[j], 1, 1) for j in order])

    def cells(gate_pre, up_pre, da):
        sig = jax.nn.sigmoid(gate_pre)
        act = (gate_pre * sig * up_pre).astype(BF)
        pair = jnp.sum(act.astype(F32) * da, axis=1, keepdims=True)
        gg = (da * up_pre * sig * (1.0 + gate_pre * (1.0 - sig))).astype(BF)
        gu = (da * gate_pre * sig).astype(BF)
        return act, pair, gg, gu

    a0, p0, gg0, gu0 = cells(pre[:, :half], pre[:, half : 2 * half], dact[:, :half])
    a1, p1, gg1, gu1 = cells(
        pre[:, 2 * half : 3 * half], pre[:, 3 * half :], dact[:, half:]
    )
    pair = p0 + p1
    pair_hi = pair.astype(BF)
    pair_lo = (pair - pair_hi.astype(F32)).astype(BF)
    place = lax.broadcasted_iota(jnp.int32, (rows, 128), 1)
    pair_cols = jnp.where(place == 0, pair_hi, jnp.where(place == 1, pair_lo, jnp.zeros((), BF)))
    grads = jnp.concatenate([gg0, gu0, gg1, gu1, pair_cols], axis=1)

    far_give = dot(grads, give[2], 1, 1).astype(BF)
    far_got = shift(far_give, "core", 1)

    def wide(g, out):
        out = out.reshape(ny, width, 2 * half)
        for j in range(ny):
            out = lax.dynamic_update_index_in_dim(
                out, dot(xs[j], g, 0, 0).astype(BF), (yi + j) % ny, 0
            )
        return out.reshape(ny * width, 2 * half)

    def down(a, out):
        for j in range(ny):
            out = lax.dynamic_update_slice_in_dim(
                out, dot(a, gs[j], 0, 0).astype(BF), ((yi + j) % ny) * width, 1
            )
        return out

    d_give = down(after(a1, far_give), down_oth)
    d_got = shift(d_give, "xl", 1)
    t_far = (dot(after(grads, d_give), keep[2], 1, 1) + far_got.astype(F32)).astype(BF)
    from_prev = shift(t_far[:h], "y", 1)
    from_next = shift(t_far[h:], "y", -1)

    later = after(grads, t_far)
    rest = jnp.concatenate([dot(later, give[j], 1, 1).astype(BF) for j in (1, 3, 0)], axis=0)
    w_give = wide(after(jnp.concatenate([gg1, gu1], axis=1), rest), wide_oth)
    w_got = shift(w_give, "xl", 1)
    rest = shift(rest, "core", 1)
    got = {
        j: rest[k * rows : (k + 1) * rows].astype(F32) for k, j in enumerate((1, 3, 0))
    }

    from_prev, from_next = lax.optimization_barrier((from_prev, from_next))
    zero = jnp.zeros((h, lanes), F32)
    later = after(grads, w_give)
    t_next = dot(later, keep[1], 1, 1) + got[1]
    t_prev = dot(later, keep[3], 1, 1) + got[3]
    t_next = (t_next + jnp.concatenate([from_prev.astype(F32), zero], axis=0)).astype(BF)
    t_prev = (t_prev + jnp.concatenate([zero, from_next.astype(F32)], axis=0)).astype(BF)
    got_a = shift(t_next, "y", 1)
    got_b = shift(t_prev, "y", -1)
    t_own = dot(grads, keep[0], 1, 1) + got[0] + got_a.astype(F32) + got_b.astype(F32)

    w_own = wide(after(jnp.concatenate([gg0, gu0], axis=1), got_a), wide_own)
    d_own = down(after(a0, got_a), down_own)
    back = lax.all_to_all(
        t_own.astype(BF).reshape(peers, cap, lanes), EX, 0, 0, tiled=True
    ).reshape(rows, lanes)

    part = dot(placing, back[:, : 2 * piece], 0, 0)
    x_own = jnp.where(xl == 0, part[:, :piece], part[:, piece:])
    x_give = jnp.where(xl == 0, part[:, piece:], part[:, :piece])
    grad_tokens = (x_own + shift(x_give, "xl", 1)).astype(BF)

    pair_back = back[:, 2 * piece : 2 * piece + 1].astype(F32)
    of_token = jnp.sum(jnp.where(match, pair_back.reshape(peers, cap, 1), 0.0), axis=1)
    pair_sum = jnp.sum(jnp.where(hit, of_token[:, None, :], 0.0), axis=0)
    pair_sum = total(pair_sum, "xl")
    grad_gates = (pair_sum / gates_t).T

    def paired(own, got):
        return jnp.stack([jnp.where(xl == 0, own, got), jnp.where(xl == 0, got, own)])

    grad_gate = paired(w_own[:, :half], w_got[:, :half])
    grad_up = paired(w_own[:, half:], w_got[:, half:])
    grad_down = paired(d_own, d_got)
    return grad_tokens, grad_gates, grad_gate, grad_up, grad_down


def solution(mesh):
    fine = Mesh(mesh.devices.reshape(4, 2, 2, 8, 2), DP + EX)
    return jax.shard_map(
        per_device,
        mesh=fine,
        in_specs=(
            P(EX, DP),
            P(EX, DP),
            P(EX, None),
            P(EX, None),
            P(EX, None, DP),
            P(EX, None, DP),
            P(EX, DP, None),
        ),
        out_specs=(
            P(EX, DP),
            P(EX, None),
            P(EX, None, DP),
            P(EX, None, DP),
            P(EX, DP, None),
        ),
        check_vma=False,
    )
```

```python
import jax
import jax.numpy as jnp
from jax import lax
from jax.sharding import Mesh, PartitionSpec as P

BF = jnp.bfloat16
F32 = jnp.float32
DP = ("y", "xl", "core")
EX = ("z", "xh")


def shift(x, axis, by):
    n = lax.axis_size(axis)
    return lax.ppermute(x, axis, [(i, (i + by) % n) for i in range(n)])


def dot(a, b, ca, cb):
    return lax.dot_general(a, b, (((ca,), (cb,)), ((), ())), preferred_element_type=F32)


def total(x, axis):
    n = lax.axis_size(axis)
    step = 1
    while step < n:
        x = x + lax.ppermute(x, axis, [(i, i ^ step) for i in range(n)])
        step *= 2
    return x


def after(x, *others):
    return lax.optimization_barrier((x,) + others)[0]


def per_device(tokens, grad_out, routing, gates, w_gate, w_up, w_down):
    toks, topk = routing.shape
    peers = lax.axis_size("z") * lax.axis_size("xh")
    experts = peers * w_gate.shape[0]
    cap = min(toks, 5 * toks * topk // (4 * experts))
    half = w_gate.shape[2]
    piece = tokens.shape[1]
    core = lax.axis_index("core")
    xl = lax.axis_index("xl")
    yi = lax.axis_index("y")
    ny = lax.axis_size("y")
    rows = peers * cap
    h = rows // 2
    width = 2 * piece

    both = jnp.concatenate([tokens, grad_out], axis=0)
    other = shift(both, "xl", 1)
    both = jnp.where(
        xl == 0,
        jnp.concatenate([both, other], axis=1),
        jnp.concatenate([other, both], axis=1),
    )

    route_t = routing.T
    gates_t = gates.T.astype(F32)
    ids = 2 * jnp.arange(peers, dtype=jnp.int32) + xl
    hit = route_t[None, :, :] == ids[:, None, None]
    chosen = jnp.any(hit, axis=1)
    gate_of = jnp.sum(jnp.where(hit, gates_t[None], 0.0), axis=1)
    upper = jnp.triu(jnp.ones((toks, toks), BF), 1)
    earlier = dot(chosen.astype(BF), upper, 1, 0).astype(jnp.int32)
    match = chosen[:, None, :] & (
        earlier[:, None, :] == jnp.arange(cap, dtype=jnp.int32)[None, :, None]
    )
    placing = match.astype(BF).reshape(rows, toks)
    weighted = jnp.where(match, gate_of[:, None, :], 0.0).astype(BF).reshape(rows, toks)

    def rows_out(sent):
        sent = sent.reshape(peers, cap, width)
        return lax.all_to_all(sent, EX, 0, 0, tiled=True).reshape(rows, width).T

    def ring(m0):
        prev = shift(m0, "y", 1)
        nxt = shift(m0, "y", -1)
        far = [shift(prev[:piece], "y", 1), shift(nxt[piece:], "y", -1)]
        ms = [m0, nxt, jnp.concatenate(far, axis=0), prev]
        return ms, [shift(m, "core", 1) for m in ms]

    def pick(w, which):
        return lax.dynamic_index_in_dim(w, which, 0, keepdims=False)

    own = [pick(w_gate, xl), pick(w_up, xl), pick(w_down, xl).T]
    give = [pick(w_gate, 1 - xl), pick(w_up, 1 - xl), pick(w_down, 1 - xl).T]

    t_sent = dot(placing, both[:toks], 1, 0).astype(BF)
    g_sent = dot(weighted, both[toks:], 1, 0).astype(BF)
    t0 = rows_out(t_sent)
    gate_oth = shift(give[0], "xl", 1)
    up_oth = shift(after(give[1], gate_oth), "xl", 1)
    down_oth = shift(after(give[2], up_oth), "xl", 1)
    tm, to = ring(t0)
    g0 = rows_out(after(g_sent, gate_oth))
    gm, go = ring(after(g0, tm[2], up_oth))

    def cut(w, j, which):
        n = w.shape[1]
        w = lax.dynamic_slice(
            w.reshape(ny, 2, 2, piece, n),
            ((yi + j) % ny, 0, which, 0, 0),
            (1, 2, 1, piece, n),
        )
        return w.reshape(width, n)

    wcat = jnp.concatenate([own[0], own[1], gate_oth, up_oth], axis=1)
    dcat = jnp.concatenate([own[2], down_oth], axis=1)
    wk = [cut(wcat, j, core) for j in range(ny)]
    wg = [cut(wcat, j, 1 - core) for j in range(ny)]
    dk = [cut(dcat, j, core) for j in range(ny)]
    dg = [cut(dcat, j, 1 - core) for j in range(ny)]
    lanes = -(-(width + 1) // 128) * 128
    row = lax.broadcasted_iota(jnp.int32, (lanes, 128), 0)
    col = lax.broadcasted_iota(jnp.int32, (lanes, 128), 1)
    extra = ((row == width) & (col < 2)).astype(BF)

    def longer(w):
        return jnp.concatenate([jnp.pad(w, ((0, lanes - width), (0, 0))), extra], axis=1)

    keep = [longer(w) for w in wk]
    give = [longer(w) for w in wg]

    def added(parts):
        s = parts[0]
        for p in parts[1:]:
            s = s + p
        return s

    order = [0, 1, 3, 2]
    pre = added([dot(tm[j], wk[j], 0, 0) + dot(to[j], wg[j], 0, 0) for j in order])
    gate_pre = jnp.concatenate([pre[:, :half], pre[:, 2 * half : 3 * half]], axis=1)
    up_pre = jnp.concatenate([pre[:, half : 2 * half], pre[:, 3 * half :]], axis=1)
    sig = jax.nn.sigmoid(gate_pre)
    act = (gate_pre * sig * up_pre).astype(BF)
    to_gate = up_pre * sig * (1.0 + gate_pre * (1.0 - sig))
    to_up = gate_pre * sig
    act, to_gate, to_up = lax.optimization_barrier((act, to_gate, to_up))

    dact = added([dot(gm[j], dk[j], 0, 0) + dot(go[j], dg[j], 0, 0) for j in order])
    pair = jnp.sum(act.astype(F32) * dact, axis=1, keepdims=True)
    gg = (dact * to_gate).astype(BF)
    gu = (dact * to_up).astype(BF)
    pair_hi = pair.astype(BF)
    pair_lo = (pair - pair_hi.astype(F32)).astype(BF)
    place = lax.broadcasted_iota(jnp.int32, (rows, 128), 1)
    pair_cols = jnp.where(place == 0, pair_hi, jnp.where(place == 1, pair_lo, jnp.zeros((), BF)))
    g_own = jnp.concatenate([gg[:, :half], gu[:, :half]], axis=1)
    g_oth = jnp.concatenate([gg[:, half:], gu[:, half:]], axis=1)
    grads = jnp.concatenate([g_own, g_oth, pair_cols], axis=1)

    def weight_grad(mine, theirs, g):
        n = g.shape[1]
        out = jnp.zeros((ny, 2, 2, piece, n), BF)
        for j in order:
            for which, x in ((core, mine[j]), (1 - core, theirs[j])):
                part = dot(x, g, 1, 0).astype(BF).reshape(1, 2, 1, piece, n)
                out = lax.dynamic_update_slice(out, part, ((yi + j) % ny, 0, which, 0, 0))
        return out.reshape(ny * 2 * width, n)

    far_give = dot(grads, give[2], 1, 1).astype(BF)
    far_got = shift(far_give, "core", 1)
    d_give = weight_grad(gm, go, act[:, half:])
    d_got = shift(d_give, "xl", 1)
    t_far = (dot(grads, keep[2], 1, 1) + far_got.astype(F32)).astype(BF)
    from_prev = shift(t_far[:h], "y", 1)
    from_next = shift(t_far[h:], "y", -1)

    later = after(grads, t_far)
    rest = jnp.concatenate([dot(later, give[j], 1, 1).astype(BF) for j in (1, 3, 0)], axis=0)
    w_give = weight_grad(tm, to, after(g_oth, rest))
    w_got = shift(w_give, "xl", 1)
    rest = shift(rest, "core", 1)
    got = {
        j: rest[k * rows : (k + 1) * rows].astype(F32) for k, j in enumerate((1, 3, 0))
    }

    from_prev, from_next = lax.optimization_barrier((from_prev, from_next))
    zero = jnp.zeros((h, lanes), F32)
    later = after(grads, w_give)
    t_next = dot(later, keep[1], 1, 1) + got[1]
    t_prev = dot(later, keep[3], 1, 1) + got[3]
    t_next = (t_next + jnp.concatenate([from_prev.astype(F32), zero], axis=0)).astype(BF)
    t_prev = (t_prev + jnp.concatenate([zero, from_next.astype(F32)], axis=0)).astype(BF)
    got_a = shift(t_next, "y", 1)
    got_b = shift(t_prev, "y", -1)
    t_own = dot(grads, keep[0], 1, 1) + got[0] + got_a.astype(F32) + got_b.astype(F32)

    w_own = weight_grad(tm, to, after(g_own, got_a))
    d_own = weight_grad(gm, go, after(act[:, :half], got_a))
    back = lax.all_to_all(
        t_own.astype(BF).reshape(peers, cap, lanes), EX, 0, 0, tiled=True
    ).reshape(rows, lanes)

    part = dot(placing, back[:, :width], 0, 0)
    x_own = jnp.where(xl == 0, part[:, :piece], part[:, piece:])
    x_give = jnp.where(xl == 0, part[:, piece:], part[:, :piece])
    grad_tokens = (x_own + shift(x_give, "xl", 1)).astype(BF)

    pair_back = back[:, width : width + 1].astype(F32)
    of_token = jnp.sum(jnp.where(match, pair_back.reshape(peers, cap, 1), 0.0), axis=1)
    pair_sum = jnp.sum(jnp.where(hit, of_token[:, None, :], 0.0), axis=0)
    pair_sum = total(pair_sum, "xl")
    grad_gates = (pair_sum / gates_t).T

    def paired(own, got):
        return jnp.stack([jnp.where(xl == 0, own, got), jnp.where(xl == 0, got, own)])

    grad_gate = paired(w_own[:, :half], w_got[:, :half])
    grad_up = paired(w_own[:, half:], w_got[:, half:])
    grad_down = paired(d_own.T, d_got.T)
    return grad_tokens, grad_gates, grad_gate, grad_up, grad_down


def solution(mesh):
    fine = Mesh(mesh.devices.reshape(4, 2, 2, 8, 2), DP + EX)
    return jax.shard_map(
        per_device,
        mesh=fine,
        in_specs=(
            P(EX, DP),
            P(EX, DP),
            P(EX, None),
            P(EX, None),
            P(EX, None, DP),
            P(EX, None, DP),
            P(EX, DP, None),
        ),
        out_specs=(
            P(EX, DP),
            P(EX, None),
            P(EX, None, DP),
            P(EX, None, DP),
            P(EX, DP, None),
        ),
        check_vma=False,
    )
```

```python
import jax
import jax.numpy as jnp
from jax import lax
from jax.sharding import Mesh, PartitionSpec as P

BF = jnp.bfloat16
F32 = jnp.float32
DP = ("y", "xl", "core")
EX = ("z", "xh")


def shift(x, axis, by):
    n = lax.axis_size(axis)
    return lax.ppermute(x, axis, [(i, (i + by) % n) for i in range(n)])


def dot(a, b, ca, cb):
    return lax.dot_general(a, b, (((ca,), (cb,)), ((), ())), preferred_element_type=F32)


def total(x, axis):
    n = lax.axis_size(axis)
    step = 1
    while step < n:
        x = x + lax.ppermute(x, axis, [(i, i ^ step) for i in range(n)])
        step *= 2
    return x


def after(x, *others):
    return lax.optimization_barrier((x,) + others)[0]


def per_device(tokens, grad_out, routing, gates, w_gate, w_up, w_down):
    toks, topk = routing.shape
    peers = lax.axis_size("z") * lax.axis_size("xh")
    experts = peers * w_gate.shape[0]
    cap = min(toks, 5 * toks * topk // (4 * experts))
    half = w_gate.shape[2]
    piece = tokens.shape[1]
    core = lax.axis_index("core")
    xl = lax.axis_index("xl")
    yi = lax.axis_index("y")
    ny = lax.axis_size("y")
    rows = peers * cap
    h = rows // 2
    width = 2 * piece

    both = jnp.concatenate([tokens, grad_out], axis=0)
    other = shift(both, "xl", 1)
    both = jnp.where(
        xl == 0,
        jnp.concatenate([both, other], axis=1),
        jnp.concatenate([other, both], axis=1),
    )

    route_t = routing.T
    gates_t = gates.T.astype(F32)
    ids = 2 * jnp.arange(peers, dtype=jnp.int32) + xl
    hit = route_t[None, :, :] == ids[:, None, None]
    chosen = jnp.any(hit, axis=1)
    gate_of = jnp.sum(jnp.where(hit, gates_t[None], 0.0), axis=1)
    upper = jnp.triu(jnp.ones((toks, toks), BF), 1)
    earlier = dot(chosen.astype(BF), upper, 1, 0).astype(jnp.int32)
    match = chosen[:, None, :] & (
        earlier[:, None, :] == jnp.arange(cap, dtype=jnp.int32)[None, :, None]
    )
    placing = match.astype(BF).reshape(rows, toks)
    weighted = jnp.where(match, gate_of[:, None, :], 0.0).astype(BF).reshape(rows, toks)

    def rows_out(sent):
        sent = sent.reshape(peers, cap, width)
        return lax.all_to_all(sent, EX, 0, 0, tiled=True).reshape(rows, width).T

    def ring(m0):
        prev = shift(m0, "y", 1)
        nxt = shift(m0, "y", -1)
        far = [shift(prev[:piece], "y", 1), shift(nxt[piece:], "y", -1)]
        ms = [m0, nxt, jnp.concatenate(far, axis=0), prev]
        return ms, [shift(m, "core", 1) for m in ms]

    def pick(w, which):
        return lax.dynamic_index_in_dim(w, which, 0, keepdims=False)

    own = [pick(w_gate, xl), pick(w_up, xl), pick(w_down, xl).T]
    give = [pick(w_gate, 1 - xl), pick(w_up, 1 - xl), pick(w_down, 1 - xl).T]

    t_sent = dot(placing, both[:toks], 1, 0).astype(BF)
    g_sent = dot(weighted, both[toks:], 1, 0).astype(BF)
    t0 = after(rows_out(t_sent), g_sent)
    gate_oth = shift(after(give[0], both), "xl", 1)
    up_oth = shift(after(give[1], gate_oth), "xl", 1)
    down_oth = shift(after(give[2], up_oth), "xl", 1)
    tm, to = ring(t0)
    g0 = rows_out(after(g_sent, gate_oth))
    gm, go = ring(after(g0, tm[2], up_oth))

    def cut(w, j, which):
        n = w.shape[1]
        w = lax.dynamic_slice(
            w.reshape(ny, 2, 2, piece, n),
            ((yi + j) % ny, 0, which, 0, 0),
            (1, 2, 1, piece, n),
        )
        return w.reshape(width, n)

    wcat = jnp.concatenate([own[0], own[1], gate_oth, up_oth], axis=1)
    dcat = jnp.concatenate([own[2], down_oth], axis=1)
    wk = [cut(wcat, j, core) for j in range(ny)]
    wg = [cut(wcat, j, 1 - core) for j in range(ny)]
    dk = [cut(dcat, j, core) for j in range(ny)]
    dg = [cut(dcat, j, 1 - core) for j in range(ny)]
    lanes = -(-(width + 1) // 128) * 128
    row = lax.broadcasted_iota(jnp.int32, (lanes, 128), 0)
    col = lax.broadcasted_iota(jnp.int32, (lanes, 128), 1)
    extra = ((row == width) & (col < 2)).astype(BF)

    def longer(w):
        return jnp.concatenate([jnp.pad(w, ((0, lanes - width), (0, 0))), extra], axis=1)

    keep = [longer(w) for w in wk]
    give = [longer(w) for w in wg]

    def added(parts):
        s = parts[0]
        for p in parts[1:]:
            s = s + p
        return s

    order = [0, 1, 3, 2]
    pre = added([dot(tm[j], wk[j], 0, 0) + dot(to[j], wg[j], 0, 0) for j in order])
    gate_pre = jnp.concatenate([pre[:, :half], pre[:, 2 * half : 3 * half]], axis=1)
    up_pre = jnp.concatenate([pre[:, half : 2 * half], pre[:, 3 * half :]], axis=1)
    sig = jax.nn.sigmoid(gate_pre)
    act = (gate_pre * sig * up_pre).astype(BF)
    to_gate = up_pre * sig * (1.0 + gate_pre * (1.0 - sig))
    to_up = gate_pre * sig
    turn = lax.broadcasted_iota(jnp.int32, (2, 2, piece, rows), 1)

    def whole(mine, theirs):
        m = mine.reshape(2, 1, piece, rows)
        t = theirs.reshape(2, 1, piece, rows)
        return jnp.where(turn == core, m, t).reshape(2 * width, rows)

    txs = [whole(tm[j], to[j]) for j in range(ny)]
    act, to_gate, to_up, txs = lax.optimization_barrier((act, to_gate, to_up, txs))

    dact = added([dot(gm[j], dk[j], 0, 0) + dot(go[j], dg[j], 0, 0) for j in order])
    pair = jnp.sum(act.astype(F32) * dact, axis=1, keepdims=True)
    gg = (dact * to_gate).astype(BF)
    gu = (dact * to_up).astype(BF)
    pair_hi = pair.astype(BF)
    pair_lo = (pair - pair_hi.astype(F32)).astype(BF)
    place = lax.broadcasted_iota(jnp.int32, (rows, 128), 1)
    pair_cols = jnp.where(place == 0, pair_hi, jnp.where(place == 1, pair_lo, jnp.zeros((), BF)))
    g_own = jnp.concatenate([gg[:, :half], gu[:, :half]], axis=1)
    g_oth = jnp.concatenate([gg[:, half:], gu[:, half:]], axis=1)
    grads = jnp.concatenate([g_own, g_oth, pair_cols], axis=1)

    def wide_grad(g):
        n = g.shape[1]
        out = jnp.zeros((ny, 2 * width, n), BF)
        for j in order:
            part = dot(txs[j], g, 1, 0).astype(BF)
            out = lax.dynamic_update_index_in_dim(out, part, (yi + j) % ny, 0)
        return out.reshape(ny * 2 * width, n)

    def down_grad(a):
        n = a.shape[1]
        out = jnp.zeros((ny, 2, 2, piece, n), BF)
        for j in order:
            for which, x in ((core, gm[j]), (1 - core, go[j])):
                part = dot(x, a, 1, 0).astype(BF).reshape(1, 2, 1, piece, n)
                out = lax.dynamic_update_slice(out, part, ((yi + j) % ny, 0, which, 0, 0))
        return out.reshape(ny * 2 * width, n)

    far_give = dot(grads, give[2], 1, 1).astype(BF)
    far_got = shift(far_give, "core", 1)
    d_give = down_grad(act[:, half:])
    d_got = shift(d_give, "xl", 1)
    t_far = (dot(grads, keep[2], 1, 1) + far_got.astype(F32)).astype(BF)
    from_prev = shift(t_far[:h], "y", 1)
    from_next = shift(t_far[h:], "y", -1)

    later = after(grads, t_far, d_give)
    rest = jnp.concatenate([dot(later, give[j], 1, 1).astype(BF) for j in (1, 3, 0)], axis=0)
    w_give = wide_grad(after(g_oth, rest))
    w_got = shift(w_give, "xl", 1)
    rest = shift(rest, "core", 1)
    got = {
        j: rest[k * rows : (k + 1) * rows].astype(F32) for k, j in enumerate((1, 3, 0))
    }

    from_prev, from_next = lax.optimization_barrier((from_prev, from_next))
    zero = jnp.zeros((h, lanes), F32)
    later = after(grads, w_give)
    t_next = dot(later, keep[1], 1, 1) + got[1]
    t_prev = dot(later, keep[3], 1, 1) + got[3]
    t_next = (t_next + jnp.concatenate([from_prev.astype(F32), zero], axis=0)).astype(BF)
    t_prev = (t_prev + jnp.concatenate([zero, from_next.astype(F32)], axis=0)).astype(BF)
    got_a = shift(t_next, "y", 1)
    got_b = shift(t_prev, "y", -1)
    t_own = dot(grads, keep[0], 1, 1) + got[0] + got_a.astype(F32) + got_b.astype(F32)

    w_own = wide_grad(after(g_own, got_a))
    d_own = down_grad(after(act[:, :half], got_a))
    back = lax.all_to_all(
        t_own.astype(BF).reshape(peers, cap, lanes), EX, 0, 0, tiled=True
    ).reshape(rows, lanes)

    part = dot(placing, back[:, :width], 0, 0)
    x_own = jnp.where(xl == 0, part[:, :piece], part[:, piece:])
    x_give = jnp.where(xl == 0, part[:, piece:], part[:, :piece])
    grad_tokens = (x_own + shift(x_give, "xl", 1)).astype(BF)

    pair_back = back[:, width : width + 1].astype(F32)
    of_token = jnp.sum(jnp.where(match, pair_back.reshape(peers, cap, 1), 0.0), axis=1)
    pair_sum = jnp.sum(jnp.where(hit, of_token[:, None, :], 0.0), axis=0)
    pair_sum = total(pair_sum, "xl")
    grad_gates = (pair_sum / gates_t).T

    def paired(own, got):
        out = jnp.zeros((2,) + own.shape, BF)
        out = lax.dynamic_update_index_in_dim(out, own, xl, 0)
        return lax.dynamic_update_index_in_dim(out, got, 1 - xl, 0)

    d_own, d_got = d_own.T, d_got.T
    grad_down = jnp.stack([jnp.where(xl == 0, d_own, d_got), jnp.where(xl == 0, d_got, d_own)])
    w_got = after(w_got, x_give, grad_down)
    grad_gate = paired(w_own[:, :half], w_got[:, :half])
    grad_up = paired(w_own[:, half:], w_got[:, half:])
    return grad_tokens, grad_gates, grad_gate, grad_up, grad_down


def solution(mesh):
    fine = Mesh(mesh.devices.reshape(4, 2, 2, 8, 2), DP + EX)
    return jax.shard_map(
        per_device,
        mesh=fine,
        in_specs=(
            P(EX, DP),
            P(EX, DP),
            P(EX, None),
            P(EX, None),
            P(EX, None, DP),
            P(EX, None, DP),
            P(EX, DP, None),
        ),
        out_specs=(
            P(EX, DP),
            P(EX, None),
            P(EX, None, DP),
            P(EX, None, DP),
            P(EX, DP, None),
        ),
        check_vma=False,
    )
```

```python
import jax
import jax.numpy as jnp
from jax import lax
from jax.sharding import Mesh, PartitionSpec as P

BF = jnp.bfloat16
F32 = jnp.float32
DP = ("y", "xl", "core")
EX = ("z", "xh")


def shift(x, axis, by):
    n = lax.axis_size(axis)
    return lax.ppermute(x, axis, [(i, (i + by) % n) for i in range(n)])


def dot(a, b, ca, cb):
    return lax.dot_general(a, b, (((ca,), (cb,)), ((), ())), preferred_element_type=F32)


def total(x, axis):
    n = lax.axis_size(axis)
    step = 1
    while step < n:
        x = x + lax.ppermute(x, axis, [(i, i ^ step) for i in range(n)])
        step *= 2
    return x


def after(x, *others):
    return lax.optimization_barrier((x,) + others)[0]


def per_device(tokens, grad_out, routing, gates, w_gate, w_up, w_down):
    toks, topk = routing.shape
    peers = lax.axis_size("z") * lax.axis_size("xh")
    experts = peers * w_gate.shape[0]
    cap = min(toks, 5 * toks * topk // (4 * experts))
    half = w_gate.shape[2]
    piece = tokens.shape[1]
    core = lax.axis_index("core")
    xl = lax.axis_index("xl")
    yi = lax.axis_index("y")
    ny = lax.axis_size("y")
    rows = peers * cap
    h = rows // 2

    both = jnp.concatenate([tokens, grad_out], axis=0)
    both = lax.all_gather(both, ("xl", "core"), axis=1, tiled=True)
    width = both.shape[1]
    mine = lax.dynamic_slice_in_dim(both, core * toks, toks, 0)

    route_t = routing.T
    gates_t = gates.T.astype(F32)
    ids = 2 * jnp.arange(peers, dtype=jnp.int32) + xl
    hit = route_t[None, :, :] == ids[:, None, None]
    chosen = jnp.any(hit, axis=1)
    gate_of = jnp.sum(jnp.where(hit, gates_t[None], 0.0), axis=1)
    upper = jnp.triu(jnp.ones((toks, toks), BF), 1)
    earlier = dot(chosen.astype(BF), upper, 1, 0).astype(jnp.int32)
    match = chosen[:, None, :] & (
        earlier[:, None, :] == jnp.arange(cap, dtype=jnp.int32)[None, :, None]
    )
    placing = match.astype(BF).reshape(rows, toks)
    scale = jnp.where(core == 0, 1.0, gate_of)
    weighted = jnp.where(match, scale[:, None, :], 0.0).astype(BF).reshape(rows, toks)

    sent = dot(weighted, mine, 1, 0).astype(BF).reshape(peers, cap, width)

    def pick(w):
        own = lax.dynamic_index_in_dim(w, xl, 0, keepdims=False)
        give = lax.dynamic_index_in_dim(w, 1 - xl, 0, keepdims=False)
        return own, shift(after(give, both), "xl", 1)

    gate_own, gate_oth = pick(w_gate)
    up_own, up_oth = pick(w_up)
    down_own, down_oth = pick(w_down)

    m0 = lax.all_to_all(sent, EX, 0, 0, tiled=True).reshape(rows, width)
    prev = shift(m0, "y", 1)
    nxt = shift(m0, "y", -1)
    far = [shift(prev[:h], "y", 1), shift(nxt[h:], "y", -1)]

    def swapped(m):
        o = shift(m, "core", 1)
        return jnp.where(core == 0, m, o), jnp.where(core == 0, o, m)

    x0, s0 = swapped(m0)
    xp, sp = swapped(prev)
    xn, sn = swapped(nxt)
    xf, sf = swapped(jnp.concatenate(far, axis=0))
    xs = [x0, xn, xf, xp]
    gs = [s0, sn, sf, sp]

    wcat = jnp.concatenate([gate_own, up_own, gate_oth, up_oth], axis=1).reshape(
        ny, width, 4 * half
    )
    wdown = jnp.concatenate([down_own, down_oth], axis=0)
    wj = [
        lax.dynamic_index_in_dim(wcat, (yi + j) % ny, 0, keepdims=False) for j in range(ny)
    ]
    dj = [
        lax.dynamic_slice_in_dim(wdown, ((yi + j) % ny) * width, width, 1) for j in range(ny)
    ]
    wparts = [w.reshape(2, 2, piece, 4 * half) for w in wj]
    lanes = -(-(2 * piece + 1) // 128) * 128
    spare = lax.broadcasted_iota(jnp.int32, (1, lanes), 1) == 2 * piece

    def halved(w, which):
        w = lax.dynamic_index_in_dim(w, which, 1, keepdims=False).reshape(2 * piece, 4 * half)
        return jnp.pad(w, ((0, lanes - 2 * piece), (0, 0)))

    keep = [halved(w, core) for w in wparts]
    give = [halved(w, 1 - core) for w in wparts]

    def added(parts):
        s = parts[0]
        for p in parts[1:]:
            s = s + p
        return s

    order = [0, 1, 3, 2]
    pre = added([dot(xs[j], wj[j], 1, 0) for j in order])
    dact = added([dot(gs[j], dj[j], 1, 1) for j in order])

    def cells(gate_pre, up_pre, da):
        sig = jax.nn.sigmoid(gate_pre)
        act = (gate_pre * sig * up_pre).astype(BF)
        pair = jnp.sum(act.astype(F32) * da, axis=1, keepdims=True)
        gg = (da * up_pre * sig * (1.0 + gate_pre * (1.0 - sig))).astype(BF)
        gu = (da * gate_pre * sig).astype(BF)
        return act, pair, gg, gu

    a0, p0, gg0, gu0 = cells(pre[:, :half], pre[:, half : 2 * half], dact[:, :half])
    a1, p1, gg1, gu1 = cells(
        pre[:, 2 * half : 3 * half], pre[:, 3 * half :], dact[:, half:]
    )
    grads = jnp.concatenate([gg0, gu0, gg1, gu1], axis=1)

    pair_row = jnp.where(spare, p0 + p1, 0.0)

    def term(g, w):
        return dot(g, w, 1, 1) + pair_row

    far_give = term(grads, give[2]).astype(BF)
    far_got = shift(far_give, "core", 1)

    def narrow(g):
        out = jnp.zeros((ny, width, g.shape[1]), BF)
        for j in range(ny):
            out = lax.dynamic_update_index_in_dim(
                out, dot(xs[j], g, 0, 0).astype(BF), (yi + j) % ny, 0
            )
        return out.reshape(ny * width, g.shape[1])

    def down(a):
        out = jnp.zeros((half, ny * width), BF)
        for j in range(ny):
            out = lax.dynamic_update_slice_in_dim(
                out, dot(a, gs[j], 0, 0).astype(BF), ((yi + j) % ny) * width, 1
            )
        return out

    d_give = down(after(a1, far_give))
    d_got = shift(d_give, "xl", 1)
    t_far = (term(after(grads, d_give), keep[2]) + far_got.astype(F32)).astype(BF)
    from_prev = shift(t_far[:h], "y", 1)
    from_next = shift(t_far[h:], "y", -1)
    later = after(grads, t_far)
    rest = jnp.concatenate([term(later, give[j]).astype(BF) for j in (1, 3, 0)], axis=0)
    rest = shift(rest, "core", 1)
    got = {
        j: rest[k * rows : (k + 1) * rows].astype(F32) for k, j in enumerate((1, 3, 0))
    }

    from_prev, from_next = lax.optimization_barrier((from_prev, from_next))
    zero = jnp.zeros((h, lanes), F32)
    t_next = term(grads, keep[1]) + got[1]
    t_prev = term(grads, keep[3]) + got[3]
    t_next = (t_next + jnp.concatenate([from_prev.astype(F32), zero], axis=0)).astype(BF)
    t_prev = (t_prev + jnp.concatenate([zero, from_next.astype(F32)], axis=0)).astype(BF)
    got_a = shift(t_next, "y", 1)
    got_b = shift(t_prev, "y", -1)
    gate_give = narrow(after(gg1, t_next, t_prev))
    gate_got = shift(gate_give, "xl", 1)
    up_give = narrow(after(gu1, gate_give, d_got))
    up_got = shift(up_give, "xl", 1)
    got_a, got_b = lax.optimization_barrier((got_a, got_b))
    t_own = term(after(grads, up_give), keep[0]) + got[0]
    t_own = (t_own + got_a.astype(F32) + got_b.astype(F32)).astype(BF)

    w_own = narrow(after(jnp.concatenate([gg0, gu0], axis=1), got_a, gate_got))
    d_own = down(after(a0, w_own))
    back = lax.all_to_all(
        t_own.reshape(peers, cap, lanes), EX, 0, 0, tiled=True
    ).reshape(rows, lanes)

    part = dot(placing, back[:, : 2 * piece], 0, 0)
    x_own = jnp.where(xl == 0, part[:, :piece], part[:, piece:])
    x_give = jnp.where(xl == 0, part[:, piece:], part[:, :piece])
    grad_tokens = (x_own + shift(x_give, "xl", 1)).astype(BF)

    pair_back = back[:, 2 * piece : 2 * piece + 1].astype(F32)
    of_token = jnp.sum(jnp.where(match, pair_back.reshape(peers, cap, 1), 0.0), axis=1)
    pair_sum = jnp.sum(jnp.where(hit, of_token[:, None, :], 0.0), axis=0)
    pair_sum = total(pair_sum, "xl")
    grad_gates = (pair_sum / gates_t).T

    def paired(own, got):
        return jnp.stack([jnp.where(xl == 0, own, got), jnp.where(xl == 0, got, own)])

    grad_gate = paired(w_own[:, :half], gate_got)
    grad_down = paired(d_own, d_got)
    up_got = after(up_got, x_give, grad_gate, grad_down)
    grad_up = paired(w_own[:, half:], up_got)
    return grad_tokens, grad_gates, grad_gate, grad_up, grad_down


def solution(mesh):
    fine = Mesh(mesh.devices.reshape(4, 2, 2, 8, 2), DP + EX)
    return jax.shard_map(
        per_device,
        mesh=fine,
        in_specs=(
            P(EX, DP),
            P(EX, DP),
            P(EX, None),
            P(EX, None),
            P(EX, None, DP),
            P(EX, None, DP),
            P(EX, DP, None),
        ),
        out_specs=(
            P(EX, DP),
            P(EX, None),
            P(EX, None, DP),
            P(EX, None, DP),
            P(EX, DP, None),
        ),
        check_vma=False,
    )
```

```python
import jax
import jax.numpy as jnp
from jax import lax
from jax.sharding import Mesh, PartitionSpec as P

BF = jnp.bfloat16
F32 = jnp.float32
DP = ("y", "xl", "core")
EX = ("z", "xh")


def shift(x, axis, by):
    n = lax.axis_size(axis)
    return lax.ppermute(x, axis, [(i, (i + by) % n) for i in range(n)])


def dot(a, b, ca, cb):
    return lax.dot_general(a, b, (((ca,), (cb,)), ((), ())), preferred_element_type=F32)


def total(x, axis):
    n = lax.axis_size(axis)
    step = 1
    while step < n:
        x = x + lax.ppermute(x, axis, [(i, i ^ step) for i in range(n)])
        step *= 2
    return x


def after(x, *others):
    return lax.optimization_barrier((x,) + others)[0]


def per_device(tokens, grad_out, routing, gates, w_gate, w_up, w_down):
    toks, topk = routing.shape
    peers = lax.axis_size("z") * lax.axis_size("xh")
    experts = peers * w_gate.shape[0]
    cap = min(toks, 5 * toks * topk // (4 * experts))
    half = w_gate.shape[2]
    piece = tokens.shape[1]
    core = lax.axis_index("core")
    xl = lax.axis_index("xl")
    yi = lax.axis_index("y")
    ny = lax.axis_size("y")
    rows = peers * cap
    h = rows // 2

    both = jnp.concatenate([tokens, grad_out], axis=0)
    both = lax.all_gather(both, ("xl", "core"), axis=1, tiled=True)
    width = both.shape[1]
    mine = lax.dynamic_slice_in_dim(both, core * toks, toks, 0)

    route_t = routing.T
    gates_t = gates.T.astype(F32)
    ids = 2 * jnp.arange(peers, dtype=jnp.int32) + xl
    hit = route_t[None, :, :] == ids[:, None, None]
    chosen = jnp.any(hit, axis=1)
    gate_of = jnp.sum(jnp.where(hit, gates_t[None], 0.0), axis=1)
    upper = jnp.triu(jnp.ones((toks, toks), BF), 1)
    earlier = dot(chosen.astype(BF), upper, 1, 0).astype(jnp.int32)
    match = chosen[:, None, :] & (
        earlier[:, None, :] == jnp.arange(cap, dtype=jnp.int32)[None, :, None]
    )
    placing = match.astype(BF).reshape(rows, toks)
    scale = jnp.where(core == 0, 1.0, gate_of)
    weighted = jnp.where(match, scale[:, None, :], 0.0).astype(BF).reshape(rows, toks)

    sent = dot(weighted, mine, 1, 0).astype(BF).reshape(peers, cap, width)

    def pick(w):
        own = lax.dynamic_index_in_dim(w, xl, 0, keepdims=False)
        give = lax.dynamic_index_in_dim(w, 1 - xl, 0, keepdims=False)
        return own, shift(after(give, both), "xl", 1)

    gate_own, gate_oth = pick(w_gate)
    up_own, up_oth = pick(w_up)
    down_own, down_oth = pick(w_down)

    m0 = lax.all_to_all(sent, EX, 0, 0, tiled=True).reshape(rows, width)
    prev = shift(m0, "y", 1)
    nxt = shift(m0, "y", -1)
    far = [shift(prev[:h], "y", 1), shift(nxt[h:], "y", -1)]

    def swapped(m):
        o = shift(m, "core", 1)
        return jnp.where(core == 0, m, o), jnp.where(core == 0, o, m)

    x0, s0 = swapped(m0)
    xp, sp = swapped(prev)
    xn, sn = swapped(nxt)
    xf, sf = swapped(jnp.concatenate(far, axis=0))
    xs = [x0, xn, xf, xp]
    gs = [s0, sn, sf, sp]

    wcat = jnp.concatenate([gate_own, up_own, gate_oth, up_oth], axis=1).reshape(
        ny, width, 4 * half
    )
    wdown = jnp.concatenate([down_own, down_oth], axis=0)
    wj = [
        lax.dynamic_index_in_dim(wcat, (yi + j) % ny, 0, keepdims=False) for j in range(ny)
    ]
    dj = [
        lax.dynamic_slice_in_dim(wdown, ((yi + j) % ny) * width, width, 1) for j in range(ny)
    ]
    wparts = [w.reshape(2, 2, piece, 4 * half) for w in wj]
    lanes = -(-(2 * piece + 1) // 128) * 128
    spare = lax.broadcasted_iota(jnp.int32, (1, lanes), 1) == 2 * piece

    def halved(w, which):
        w = lax.dynamic_index_in_dim(w, which, 1, keepdims=False).reshape(2 * piece, 4 * half)
        return jnp.pad(w, ((0, lanes - 2 * piece), (0, 0)))

    keep = [halved(w, core) for w in wparts]
    give = [halved(w, 1 - core) for w in wparts]

    def added(parts):
        s = parts[0]
        for p in parts[1:]:
            s = s + p
        return s

    order = [0, 1, 3, 2]
    pre = added([dot(xs[j], wj[j], 1, 0) for j in order])
    dact = added([dot(gs[j], dj[j], 1, 1) for j in order])

    def cells(gate_pre, up_pre, da):
        sig = jax.nn.sigmoid(gate_pre)
        act = (gate_pre * sig * up_pre).astype(BF)
        pair = jnp.sum(act.astype(F32) * da, axis=1, keepdims=True)
        gg = (da * up_pre * sig * (1.0 + gate_pre * (1.0 - sig))).astype(BF)
        gu = (da * gate_pre * sig).astype(BF)
        return act, pair, gg, gu

    a0, p0, gg0, gu0 = cells(pre[:, :half], pre[:, half : 2 * half], dact[:, :half])
    a1, p1, gg1, gu1 = cells(
        pre[:, 2 * half : 3 * half], pre[:, 3 * half :], dact[:, half:]
    )
    grads = jnp.concatenate([gg0, gu0, gg1, gu1], axis=1)

    pair_row = jnp.where(spare, p0 + p1, 0.0)

    def term(g, w):
        return dot(g, w, 1, 1) + pair_row

    far_give = term(grads, give[2]).astype(BF)
    far_got = shift(far_give, "core", 1)

    def narrow(g):
        out = jnp.zeros((ny, width, g.shape[1]), BF)
        for j in range(ny):
            out = lax.dynamic_update_index_in_dim(
                out, dot(xs[j], g, 0, 0).astype(BF), (yi + j) % ny, 0
            )
        return out.reshape(ny * width, g.shape[1])

    def down(a):
        out = jnp.zeros((half, ny * width), BF)
        for j in range(ny):
            out = lax.dynamic_update_slice_in_dim(
                out, dot(a, gs[j], 0, 0).astype(BF), ((yi + j) % ny) * width, 1
            )
        return out

    d_give = down(after(a1, far_give))
    d_got = shift(d_give, "xl", 1)
    t_far = (term(after(grads, d_give), keep[2]) + far_got.astype(F32)).astype(BF)
    from_prev = shift(t_far[:h], "y", 1)
    from_next = shift(t_far[h:], "y", -1)
    gate_give = narrow(after(gg1, t_far))
    gate_got = shift(gate_give, "xl", 1)

    from_prev, from_next = lax.optimization_barrier((from_prev, from_next))
    later = after(grads, from_prev)
    rest = jnp.concatenate([term(later, give[j]).astype(BF) for j in (1, 3)], axis=0)
    own_give = term(after(grads, rest), give[0]).astype(BF)
    rest = shift(rest, "core", 1)
    got = {
        1: rest[:rows].astype(F32),
        3: rest[rows:].astype(F32),
        0: shift(own_give, "core", 1).astype(F32),
    }

    zero = jnp.zeros((h, lanes), F32)
    t_next = term(grads, keep[1]) + got[1]
    t_prev = term(grads, keep[3]) + got[3]
    t_next = (t_next + jnp.concatenate([from_prev.astype(F32), zero], axis=0)).astype(BF)
    t_prev = (t_prev + jnp.concatenate([zero, from_next.astype(F32)], axis=0)).astype(BF)
    got_a = shift(t_next, "y", 1)
    got_b = shift(t_prev, "y", -1)
    up_give = narrow(after(gu1, t_next, t_prev, d_got))
    up_got = shift(up_give, "xl", 1)
    got_a, got_b = lax.optimization_barrier((got_a, got_b))
    t_own = term(after(grads, up_give), keep[0]) + got[0]
    t_own = (t_own + got_a.astype(F32) + got_b.astype(F32)).astype(BF)

    w_own = narrow(after(jnp.concatenate([gg0, gu0], axis=1), got_a, gate_got))
    d_own = down(after(a0, w_own))
    back = lax.all_to_all(
        t_own.reshape(peers, cap, lanes), EX, 0, 0, tiled=True
    ).reshape(rows, lanes)

    part = dot(placing, back[:, : 2 * piece], 0, 0)
    x_own = jnp.where(xl == 0, part[:, :piece], part[:, piece:])
    x_give = jnp.where(xl == 0, part[:, piece:], part[:, :piece])
    grad_tokens = (x_own + shift(x_give, "xl", 1)).astype(BF)

    pair_back = back[:, 2 * piece : 2 * piece + 1].astype(F32)
    of_token = jnp.sum(jnp.where(match, pair_back.reshape(peers, cap, 1), 0.0), axis=1)
    pair_sum = jnp.sum(jnp.where(hit, of_token[:, None, :], 0.0), axis=0)
    pair_sum = total(pair_sum, "xl")
    grad_gates = (pair_sum / gates_t).T

    def paired(own, got):
        return jnp.stack([jnp.where(xl == 0, own, got), jnp.where(xl == 0, got, own)])

    grad_gate = paired(w_own[:, :half], gate_got)
    grad_down = paired(d_own, d_got)
    up_got = after(up_got, x_give, grad_gate, grad_down)
    grad_up = paired(w_own[:, half:], up_got)
    return grad_tokens, grad_gates, grad_gate, grad_up, grad_down


def solution(mesh):
    fine = Mesh(mesh.devices.reshape(4, 2, 2, 8, 2), DP + EX)
    return jax.shard_map(
        per_device,
        mesh=fine,
        in_specs=(
            P(EX, DP),
            P(EX, DP),
            P(EX, None),
            P(EX, None),
            P(EX, None, DP),
            P(EX, None, DP),
            P(EX, DP, None),
        ),
        out_specs=(
            P(EX, DP),
            P(EX, None),
            P(EX, None, DP),
            P(EX, None, DP),
            P(EX, DP, None),
        ),
        check_vma=False,
    )
```

```python
import jax
import jax.numpy as jnp
from jax import lax
from jax.sharding import Mesh, PartitionSpec as P

BF = jnp.bfloat16
F32 = jnp.float32
DP = ("y", "xl", "core")
EX = ("z", "xh")


def shift(x, axis, by):
    n = lax.axis_size(axis)
    return lax.ppermute(x, axis, [(i, (i + by) % n) for i in range(n)])


def dot(a, b, ca, cb):
    return lax.dot_general(a, b, (((ca,), (cb,)), ((), ())), preferred_element_type=F32)


def total(x, axis):
    n = lax.axis_size(axis)
    step = 1
    while step < n:
        x = x + lax.ppermute(x, axis, [(i, i ^ step) for i in range(n)])
        step *= 2
    return x


def after(x, *others):
    return lax.optimization_barrier((x,) + others)[0]


def per_device(tokens, grad_out, routing, gates, w_gate, w_up, w_down):
    toks, topk = routing.shape
    peers = lax.axis_size("z") * lax.axis_size("xh")
    experts = peers * w_gate.shape[0]
    cap = min(toks, 5 * toks * topk // (4 * experts))
    half = w_gate.shape[2]
    piece = tokens.shape[1]
    core = lax.axis_index("core")
    xl = lax.axis_index("xl")
    yi = lax.axis_index("y")
    ny = lax.axis_size("y")
    rows = peers * cap
    h = rows // 2

    ours = jnp.where(core == 0, tokens, grad_out)
    theirs = shift(jnp.where(core == 0, grad_out, tokens), "core", 1)

    def side(mine, got, flag):
        return jnp.where(
            flag == 0,
            jnp.concatenate([mine, got], axis=1),
            jnp.concatenate([got, mine], axis=1),
        )

    mine = side(ours, theirs, core)
    both = shift(mine, "xl", 1)
    mine = side(mine, both, xl)
    width = mine.shape[1]

    route_t = routing.T
    gates_t = gates.T.astype(F32)
    ids = 2 * jnp.arange(peers, dtype=jnp.int32) + xl
    hit = route_t[None, :, :] == ids[:, None, None]
    chosen = jnp.any(hit, axis=1)
    gate_of = jnp.sum(jnp.where(hit, gates_t[None], 0.0), axis=1)
    upper = jnp.triu(jnp.ones((toks, toks), BF), 1)
    earlier = dot(chosen.astype(BF), upper, 1, 0).astype(jnp.int32)
    match = chosen[:, None, :] & (
        earlier[:, None, :] == jnp.arange(cap, dtype=jnp.int32)[None, :, None]
    )
    placing = match.astype(BF).reshape(rows, toks)
    scale = jnp.where(core == 0, 1.0, gate_of)
    weighted = jnp.where(match, scale[:, None, :], 0.0).astype(BF).reshape(rows, toks)

    sent = dot(weighted, mine, 1, 0).astype(BF).reshape(peers, cap, width)

    def pick(w):
        own = lax.dynamic_index_in_dim(w, xl, 0, keepdims=False)
        give = lax.dynamic_index_in_dim(w, 1 - xl, 0, keepdims=False)
        return own, shift(after(give, both), "xl", 1)

    gate_own, gate_oth = pick(w_gate)
    up_own, up_oth = pick(w_up)
    down_own, down_oth = pick(w_down)

    m0 = lax.all_to_all(sent, EX, 0, 0, tiled=True).reshape(rows, width)
    prev = shift(m0, "y", 1)
    nxt = shift(m0, "y", -1)
    far = [shift(prev[:h], "y", 1), shift(nxt[h:], "y", -1)]

    def swapped(m):
        o = shift(m, "core", 1)
        return jnp.where(core == 0, m, o), jnp.where(core == 0, o, m)

    x0, s0 = swapped(m0)
    xp, sp = swapped(prev)
    xn, sn = swapped(nxt)
    xf, sf = swapped(jnp.concatenate(far, axis=0))
    xs = [x0, xn, xf, xp]
    gs = [s0, sn, sf, sp]

    wcat = jnp.concatenate([gate_own, up_own, gate_oth, up_oth], axis=1).reshape(
        ny, width, 4 * half
    )
    wdown = jnp.concatenate([down_own, down_oth], axis=0)
    wj = [
        lax.dynamic_index_in_dim(wcat, (yi + j) % ny, 0, keepdims=False) for j in range(ny)
    ]
    dj = [
        lax.dynamic_slice_in_dim(wdown, ((yi + j) % ny) * width, width, 1) for j in range(ny)
    ]
    wparts = [w.reshape(2, 2, piece, 4 * half) for w in wj]
    lanes = -(-(2 * piece + 1) // 128) * 128
    spare = lax.broadcasted_iota(jnp.int32, (1, lanes), 1) == 2 * piece

    def halved(w, which):
        w = lax.dynamic_index_in_dim(w, which, 1, keepdims=False).reshape(2 * piece, 4 * half)
        return jnp.pad(w, ((0, lanes - 2 * piece), (0, 0)))

    keep = [halved(w, core) for w in wparts]
    give = [halved(w, 1 - core) for w in wparts]

    def added(parts):
        s = parts[0]
        for p in parts[1:]:
            s = s + p
        return s

    order = [0, 1, 3, 2]
    pre = added([dot(xs[j], wj[j], 1, 0) for j in order])
    dact = added([dot(gs[j], dj[j], 1, 1) for j in order])

    def cells(gate_pre, up_pre, da):
        sig = jax.nn.sigmoid(gate_pre)
        act = (gate_pre * sig * up_pre).astype(BF)
        pair = jnp.sum(act.astype(F32) * da, axis=1, keepdims=True)
        gg = (da * up_pre * sig * (1.0 + gate_pre * (1.0 - sig))).astype(BF)
        gu = (da * gate_pre * sig).astype(BF)
        return act, pair, gg, gu

    a0, p0, gg0, gu0 = cells(pre[:, :half], pre[:, half : 2 * half], dact[:, :half])
    a1, p1, gg1, gu1 = cells(
        pre[:, 2 * half : 3 * half], pre[:, 3 * half :], dact[:, half:]
    )
    grads = jnp.concatenate([gg0, gu0, gg1, gu1], axis=1)

    pair_row = jnp.where(spare, p0 + p1, 0.0)

    def term(g, w):
        return dot(g, w, 1, 1) + pair_row

    far_give = term(grads, give[2]).astype(BF)
    far_got = shift(far_give, "core", 1)

    def narrow(g):
        out = jnp.zeros((ny, width, g.shape[1]), BF)
        for j in range(ny):
            out = lax.dynamic_update_index_in_dim(
                out, dot(xs[j], g, 0, 0).astype(BF), (yi + j) % ny, 0
            )
        return out.reshape(ny * width, g.shape[1])

    def down(a):
        out = jnp.zeros((half, ny * width), BF)
        for j in range(ny):
            out = lax.dynamic_update_slice_in_dim(
                out, dot(a, gs[j], 0, 0).astype(BF), ((yi + j) % ny) * width, 1
            )
        return out

    d_give = down(after(a1, far_give))
    d_got = shift(d_give, "xl", 1)
    t_far = (term(after(grads, d_give), keep[2]) + far_got.astype(F32)).astype(BF)
    from_prev = shift(t_far[:h], "y", 1)
    from_next = shift(t_far[h:], "y", -1)
    gate_give = narrow(after(gg1, t_far))
    gate_got = shift(gate_give, "xl", 1)

    from_prev, from_next = lax.optimization_barrier((from_prev, from_next))
    later = after(grads, from_prev)
    rest = jnp.concatenate([term(later, give[j]).astype(BF) for j in (1, 3)], axis=0)
    own_give = term(after(grads, rest), give[0]).astype(BF)
    rest = shift(rest, "core", 1)
    got = {
        1: rest[:rows].astype(F32),
        3: rest[rows:].astype(F32),
        0: shift(own_give, "core", 1).astype(F32),
    }

    zero = jnp.zeros((h, lanes), F32)
    t_next = term(grads, keep[1]) + got[1]
    t_prev = term(grads, keep[3]) + got[3]
    t_next = (t_next + jnp.concatenate([from_prev.astype(F32), zero], axis=0)).astype(BF)
    t_prev = (t_prev + jnp.concatenate([zero, from_next.astype(F32)], axis=0)).astype(BF)
    got_a = shift(t_next, "y", 1)
    got_b = shift(t_prev, "y", -1)
    up_give = narrow(after(gu1, t_next, t_prev, d_got))
    up_got = shift(up_give, "xl", 1)
    got_a, got_b = lax.optimization_barrier((got_a, got_b))
    t_own = term(after(grads, up_give), keep[0]) + got[0]
    t_own = (t_own + got_a.astype(F32) + got_b.astype(F32)).astype(BF)

    w_own = narrow(after(jnp.concatenate([gg0, gu0], axis=1), got_a, gate_got))
    d_own = down(after(a0, w_own))
    back = lax.all_to_all(
        t_own.reshape(peers, cap, lanes), EX, 0, 0, tiled=True
    ).reshape(rows, lanes)

    part = dot(placing, back[:, : 2 * piece], 0, 0)
    x_own = jnp.where(xl == 0, part[:, :piece], part[:, piece:])
    x_give = jnp.where(xl == 0, part[:, piece:], part[:, :piece])
    grad_tokens = (x_own + shift(x_give, "xl", 1)).astype(BF)

    pair_back = back[:, 2 * piece : 2 * piece + 1].astype(F32)
    of_token = jnp.sum(jnp.where(match, pair_back.reshape(peers, cap, 1), 0.0), axis=1)
    pair_sum = jnp.sum(jnp.where(hit, of_token[:, None, :], 0.0), axis=0)
    pair_sum = total(pair_sum, "xl")
    grad_gates = (pair_sum / gates_t).T

    def paired(own, got):
        return jnp.stack([jnp.where(xl == 0, own, got), jnp.where(xl == 0, got, own)])

    grad_gate = paired(w_own[:, :half], gate_got)
    grad_down = paired(d_own, d_got)
    up_got = after(up_got, x_give, grad_gate, grad_down)
    grad_up = paired(w_own[:, half:], up_got)
    return grad_tokens, grad_gates, grad_gate, grad_up, grad_down


def solution(mesh):
    fine = Mesh(mesh.devices.reshape(4, 2, 2, 8, 2), DP + EX)
    return jax.shard_map(
        per_device,
        mesh=fine,
        in_specs=(
            P(EX, DP),
            P(EX, DP),
            P(EX, None),
            P(EX, None),
            P(EX, None, DP),
            P(EX, None, DP),
            P(EX, DP, None),
        ),
        out_specs=(
            P(EX, DP),
            P(EX, None),
            P(EX, None, DP),
            P(EX, None, DP),
            P(EX, DP, None),
        ),
        check_vma=False,
    )
```

```python
import jax
import jax.numpy as jnp
from jax import lax
from jax.sharding import Mesh, PartitionSpec as P

BF = jnp.bfloat16
F32 = jnp.float32
DP = ("y", "xl", "core")
EX = ("z", "xh")


def shift(x, axis, by):
    n = lax.axis_size(axis)
    return lax.ppermute(x, axis, [(i, (i + by) % n) for i in range(n)])


def dot(a, b, ca, cb):
    return lax.dot_general(a, b, (((ca,), (cb,)), ((), ())), preferred_element_type=F32)


def total(x, axis):
    n = lax.axis_size(axis)
    step = 1
    while step < n:
        x = x + lax.ppermute(x, axis, [(i, i ^ step) for i in range(n)])
        step *= 2
    return x


def after(x, *others):
    return lax.optimization_barrier((x,) + others)[0]


def per_device(tokens, grad_out, routing, gates, w_gate, w_up, w_down):
    toks, topk = routing.shape
    peers = lax.axis_size("z") * lax.axis_size("xh")
    experts = peers * w_gate.shape[0]
    cap = min(toks, 5 * toks * topk // (4 * experts))
    half = w_gate.shape[2]
    piece = tokens.shape[1]
    core = lax.axis_index("core")
    xl = lax.axis_index("xl")
    yi = lax.axis_index("y")
    ny = lax.axis_size("y")
    rows = peers * cap
    h = rows // 2

    ours = jnp.where(core == 0, tokens, grad_out)
    theirs = shift(jnp.where(core == 0, grad_out, tokens), "core", 1)

    def side(mine, got, flag):
        return jnp.where(
            flag == 0,
            jnp.concatenate([mine, got], axis=1),
            jnp.concatenate([got, mine], axis=1),
        )

    mine = side(ours, theirs, core)
    both = shift(mine, "xl", 1)
    mine = side(mine, both, xl)
    width = mine.shape[1]

    route_t = routing.T
    gates_t = gates.T.astype(F32)
    ids = 2 * jnp.arange(peers, dtype=jnp.int32) + xl
    hit = route_t[None, :, :] == ids[:, None, None]
    chosen = jnp.any(hit, axis=1)
    gate_of = jnp.sum(jnp.where(hit, gates_t[None], 0.0), axis=1)
    upper = jnp.triu(jnp.ones((toks, toks), BF), 1)
    earlier = dot(chosen.astype(BF), upper, 1, 0).astype(jnp.int32)
    match = chosen[:, None, :] & (
        earlier[:, None, :] == jnp.arange(cap, dtype=jnp.int32)[None, :, None]
    )
    placing = match.astype(BF).reshape(rows, toks)
    scale = jnp.where(core == 0, 1.0, gate_of)
    weighted = jnp.where(match, scale[:, None, :], 0.0).astype(BF).reshape(rows, toks)

    sent = dot(weighted, mine, 1, 0).astype(BF).reshape(peers, cap, width)

    def pick(w):
        own = lax.dynamic_index_in_dim(w, xl, 0, keepdims=False)
        give = lax.dynamic_index_in_dim(w, 1 - xl, 0, keepdims=False)
        return own, shift(after(give, both), "xl", 1)

    gate_own, gate_oth = pick(w_gate)
    up_own, up_oth = pick(w_up)
    down_own, down_oth = pick(w_down)

    m0 = lax.all_to_all(sent, EX, 0, 0, tiled=True).reshape(rows, width)
    prev = shift(m0, "y", 1)
    nxt = shift(m0, "y", -1)
    far = [shift(prev[:h], "y", 1), shift(nxt[h:], "y", -1)]

    def swapped(m):
        o = shift(m, "core", 1)
        return jnp.where(core == 0, m, o), jnp.where(core == 0, o, m)

    x0, s0 = swapped(m0)
    xp, sp = swapped(prev)
    xn, sn = swapped(nxt)
    down_oth = after(down_oth, xp, sp, xn, sn)
    xf, sf = swapped(jnp.concatenate(far, axis=0))
    xs = [x0, xn, xf, xp]
    gs = [s0, sn, sf, sp]

    wcat = jnp.concatenate([gate_own, up_own, gate_oth, up_oth], axis=1).reshape(
        ny, width, 4 * half
    )
    wdown = jnp.concatenate([down_own, down_oth], axis=0)
    wj = [
        lax.dynamic_index_in_dim(wcat, (yi + j) % ny, 0, keepdims=False) for j in range(ny)
    ]
    dj = [
        lax.dynamic_slice_in_dim(wdown, ((yi + j) % ny) * width, width, 1) for j in range(ny)
    ]
    wparts = [w.reshape(2, 2, piece, 4 * half) for w in wj]
    lanes = -(-(2 * piece + 1) // 128) * 128
    spare = lax.broadcasted_iota(jnp.int32, (1, lanes), 1) == 2 * piece

    def halved(w, which):
        w = lax.dynamic_index_in_dim(w, which, 1, keepdims=False).reshape(2 * piece, 4 * half)
        return jnp.pad(w, ((0, lanes - 2 * piece), (0, 0)))

    keep = [halved(w, core) for w in wparts]
    give = [halved(w, 1 - core) for w in wparts]

    def added(parts):
        s = parts[0]
        for p in parts[1:]:
            s = s + p
        return s

    order = [0, 1, 3, 2]
    pre = added([dot(xs[j], wj[j], 1, 0) for j in order])
    dact = added([dot(gs[j], dj[j], 1, 1) for j in order])

    def cells(gate_pre, up_pre, da):
        sig = jax.nn.sigmoid(gate_pre)
        act = (gate_pre * sig * up_pre).astype(BF)
        pair = jnp.sum(act.astype(F32) * da, axis=1, keepdims=True)
        gg = (da * up_pre * sig * (1.0 + gate_pre * (1.0 - sig))).astype(BF)
        gu = (da * gate_pre * sig).astype(BF)
        return act, pair, gg, gu

    a0, p0, gg0, gu0 = cells(pre[:, :half], pre[:, half : 2 * half], dact[:, :half])
    a1, p1, gg1, gu1 = cells(
        pre[:, 2 * half : 3 * half], pre[:, 3 * half :], dact[:, half:]
    )
    grads = jnp.concatenate([gg0, gu0, gg1, gu1], axis=1)

    pair_row = jnp.where(spare, p0 + p1, 0.0)

    def term(g, w):
        return dot(g, w, 1, 1) + pair_row

    far_give = term(grads, give[2]).astype(BF)
    far_got = shift(far_give, "core", 1)

    def narrow(g):
        out = jnp.zeros((ny, width, g.shape[1]), BF)
        for j in range(ny):
            out = lax.dynamic_update_index_in_dim(
                out, dot(xs[j], g, 0, 0).astype(BF), (yi + j) % ny, 0
            )
        return out.reshape(ny * width, g.shape[1])

    def down(a):
        out = jnp.zeros((half, ny * width), BF)
        for j in range(ny):
            out = lax.dynamic_update_slice_in_dim(
                out, dot(a, gs[j], 0, 0).astype(BF), ((yi + j) % ny) * width, 1
            )
        return out

    d_give = down(after(a1, far_give))
    d_got = shift(d_give, "xl", 1)
    t_far = (term(after(grads, d_give), keep[2]) + far_got.astype(F32)).astype(BF)
    from_prev = shift(t_far[:h], "y", 1)
    from_next = shift(t_far[h:], "y", -1)
    gate_give = narrow(after(gg1, t_far))
    gate_got = shift(gate_give, "xl", 1)

    from_prev, from_next = lax.optimization_barrier((from_prev, from_next))
    later = after(grads, from_prev)
    rest = jnp.concatenate([term(later, give[j]).astype(BF) for j in (1, 3)], axis=0)
    own_give = term(after(grads, rest), give[0]).astype(BF)
    rest = shift(rest, "core", 1)
    got = {
        1: rest[:rows].astype(F32),
        3: rest[rows:].astype(F32),
        0: shift(own_give, "core", 1).astype(F32),
    }

    zero = jnp.zeros((h, lanes), F32)
    t_next = term(grads, keep[1]) + got[1]
    t_prev = term(grads, keep[3]) + got[3]
    t_next = (t_next + jnp.concatenate([from_prev.astype(F32), zero], axis=0)).astype(BF)
    t_prev = (t_prev + jnp.concatenate([zero, from_next.astype(F32)], axis=0)).astype(BF)
    got_a = shift(t_next, "y", 1)
    got_b = shift(t_prev, "y", -1)
    up_give = narrow(after(gu1, t_next, t_prev, d_got))
    up_got = shift(up_give, "xl", 1)
    got_a, got_b = lax.optimization_barrier((got_a, got_b))
    t_own = term(after(grads, up_give), keep[0]) + got[0]
    t_own = (t_own + got_a.astype(F32) + got_b.astype(F32)).astype(BF)

    w_own = narrow(after(jnp.concatenate([gg0, gu0], axis=1), got_a, gate_got))
    d_own = down(after(a0, w_own))
    back = lax.all_to_all(
        t_own.reshape(peers, cap, lanes), EX, 0, 0, tiled=True
    ).reshape(rows, lanes)

    part = dot(placing, back[:, : 2 * piece], 0, 0)
    x_own = jnp.where(xl == 0, part[:, :piece], part[:, piece:])
    x_give = jnp.where(xl == 0, part[:, piece:], part[:, :piece])
    grad_tokens = (x_own + shift(x_give, "xl", 1)).astype(BF)

    pair_back = back[:, 2 * piece : 2 * piece + 1].astype(F32)
    of_token = jnp.sum(jnp.where(match, pair_back.reshape(peers, cap, 1), 0.0), axis=1)
    pair_sum = jnp.sum(jnp.where(hit, of_token[:, None, :], 0.0), axis=0)
    pair_sum = total(pair_sum, "xl")
    grad_gates = (pair_sum / gates_t).T

    def paired(own, got):
        return jnp.stack([jnp.where(xl == 0, own, got), jnp.where(xl == 0, got, own)])

    grad_gate = paired(w_own[:, :half], gate_got)
    grad_down = paired(d_own, d_got)
    up_got = after(up_got, x_give, grad_gate, grad_down)
    grad_up = paired(w_own[:, half:], up_got)
    return grad_tokens, grad_gates, grad_gate, grad_up, grad_down


def solution(mesh):
    fine = Mesh(mesh.devices.reshape(4, 2, 2, 8, 2), DP + EX)
    return jax.shard_map(
        per_device,
        mesh=fine,
        in_specs=(
            P(EX, DP),
            P(EX, DP),
            P(EX, None),
            P(EX, None),
            P(EX, None, DP),
            P(EX, None, DP),
            P(EX, DP, None),
        ),
        out_specs=(
            P(EX, DP),
            P(EX, None),
            P(EX, None, DP),
            P(EX, None, DP),
            P(EX, DP, None),
        ),
        check_vma=False,
    )
```

```python
import jax
import jax.numpy as jnp
from jax import lax
from jax.sharding import Mesh, PartitionSpec as P

BF = jnp.bfloat16
F32 = jnp.float32
DP = ("y", "xl", "core")
EX = ("z", "xh")


def shift(x, axis, by):
    n = lax.axis_size(axis)
    return lax.ppermute(x, axis, [(i, (i + by) % n) for i in range(n)])


def dot(a, b, ca, cb):
    return lax.dot_general(a, b, (((ca,), (cb,)), ((), ())), preferred_element_type=F32)


def total(x, axis):
    n = lax.axis_size(axis)
    step = 1
    while step < n:
        x = x + lax.ppermute(x, axis, [(i, i ^ step) for i in range(n)])
        step *= 2
    return x


def after(x, *others):
    return lax.optimization_barrier((x,) + others)[0]


def per_device(tokens, grad_out, routing, gates, w_gate, w_up, w_down):
    toks, topk = routing.shape
    peers = lax.axis_size("z") * lax.axis_size("xh")
    experts = peers * w_gate.shape[0]
    cap = min(toks, 5 * toks * topk // (4 * experts))
    half = w_gate.shape[2]
    piece = tokens.shape[1]
    core = lax.axis_index("core")
    xl = lax.axis_index("xl")
    yi = lax.axis_index("y")
    ny = lax.axis_size("y")
    rows = peers * cap
    h = rows // 2

    ours = jnp.where(core == 0, tokens, grad_out)
    theirs = shift(jnp.where(core == 0, grad_out, tokens), "core", 1)

    def side(mine, got, flag):
        return jnp.where(
            flag == 0,
            jnp.concatenate([mine, got], axis=1),
            jnp.concatenate([got, mine], axis=1),
        )

    mine = side(ours, theirs, core)
    both = shift(mine, "xl", 1)
    mine = side(mine, both, xl)
    width = mine.shape[1]

    route_t = routing.T
    gates_t = gates.T.astype(F32)
    ids = 2 * jnp.arange(peers, dtype=jnp.int32) + xl
    hit = route_t[None, :, :] == ids[:, None, None]
    chosen = jnp.any(hit, axis=1)
    gate_of = jnp.sum(jnp.where(hit, gates_t[None], 0.0), axis=1)
    upper = jnp.triu(jnp.ones((toks, toks), BF), 1)
    earlier = dot(chosen.astype(BF), upper, 1, 0).astype(jnp.int32)
    match = chosen[:, None, :] & (
        earlier[:, None, :] == jnp.arange(cap, dtype=jnp.int32)[None, :, None]
    )
    placing = match.astype(BF).reshape(rows, toks)
    scale = jnp.where(core == 0, 1.0, gate_of)
    weighted = jnp.where(match, scale[:, None, :], 0.0).astype(BF).reshape(rows, toks)

    sent = dot(weighted, mine, 1, 0).astype(BF).reshape(peers, cap, width)

    def pick(w):
        own = lax.dynamic_index_in_dim(w, xl, 0, keepdims=False)
        give = lax.dynamic_index_in_dim(w, 1 - xl, 0, keepdims=False)
        return own, shift(after(give, both), "xl", 1)

    gate_own, gate_oth = pick(w_gate)
    up_own, up_oth = pick(w_up)
    down_own, down_oth = pick(w_down)

    m0 = lax.all_to_all(sent, EX, 0, 0, tiled=True).reshape(rows, width)
    prev = shift(m0, "y", 1)
    nxt = shift(m0, "y", -1)
    far = [shift(prev[:h], "y", 1), shift(nxt[h:], "y", -1)]

    def swapped(m):
        o = shift(m, "core", 1)
        return jnp.where(core == 0, m, o), jnp.where(core == 0, o, m)

    x0, s0 = swapped(m0)
    xp, sp = swapped(prev)
    xn, sn = swapped(nxt)
    xf, sf = swapped(jnp.concatenate(far, axis=0))
    xs = [x0, xn, xf, xp]
    gs = [s0, sn, sf, sp]

    wcat = jnp.concatenate([gate_own, up_own, gate_oth, up_oth], axis=1).reshape(
        ny, width, 4 * half
    )
    wdown = jnp.concatenate([down_own, down_oth], axis=0)
    wj = [
        lax.dynamic_index_in_dim(wcat, (yi + j) % ny, 0, keepdims=False) for j in range(ny)
    ]
    dj = [
        lax.dynamic_slice_in_dim(wdown, ((yi + j) % ny) * width, width, 1) for j in range(ny)
    ]
    wparts = [w.reshape(2, 2, piece, 4 * half) for w in wj]
    lanes = -(-(2 * piece + 1) // 128) * 128
    spare = lax.broadcasted_iota(jnp.int32, (1, lanes), 1) == 2 * piece

    def halved(w, which):
        w = lax.dynamic_index_in_dim(w, which, 1, keepdims=False).reshape(2 * piece, 4 * half)
        return jnp.pad(w, ((0, lanes - 2 * piece), (0, 0)))

    keep = [halved(w, core) for w in wparts]
    give = [halved(w, 1 - core) for w in wparts]

    def added(parts):
        s = parts[0]
        for p in parts[1:]:
            s = s + p
        return s

    order = [0, 1, 3, 2]
    pre = added([dot(xs[j], wj[j], 1, 0) for j in order])
    dact = added([dot(gs[j], dj[j], 1, 1) for j in order])

    def cells(gate_pre, up_pre, da):
        sig = jax.nn.sigmoid(gate_pre)
        act = (gate_pre * sig * up_pre).astype(BF)
        pair = jnp.sum(act.astype(F32) * da, axis=1, keepdims=True)
        gg = (da * up_pre * sig * (1.0 + gate_pre * (1.0 - sig))).astype(BF)
        gu = (da * gate_pre * sig).astype(BF)
        return act, pair, gg, gu

    a0, p0, gg0, gu0 = cells(pre[:, :half], pre[:, half : 2 * half], dact[:, :half])
    a1, p1, gg1, gu1 = cells(
        pre[:, 2 * half : 3 * half], pre[:, 3 * half :], dact[:, half:]
    )
    grads = jnp.concatenate([gg0, gu0, gg1, gu1], axis=1)

    pair_row = jnp.where(spare, p0 + p1, 0.0)

    def term(g, w):
        return dot(g, w, 1, 1) + pair_row

    far_give = term(grads, give[2]).astype(BF)
    far_got = shift(far_give, "core", 1)

    def narrow(g):
        out = jnp.zeros((ny, width, g.shape[1]), BF)
        for j in range(ny):
            out = lax.dynamic_update_index_in_dim(
                out, dot(xs[j], g, 0, 0).astype(BF), (yi + j) % ny, 0
            )
        return out.reshape(ny * width, g.shape[1])

    def down(a):
        out = jnp.zeros((half, ny * width), BF)
        for j in range(ny):
            out = lax.dynamic_update_slice_in_dim(
                out, dot(a, gs[j], 0, 0).astype(BF), ((yi + j) % ny) * width, 1
            )
        return out

    d_give = down(after(a1, far_give))
    d_got = shift(d_give, "xl", 1)
    t_far = (term(after(grads, d_give), keep[2]) + far_got.astype(F32)).astype(BF)
    from_prev = shift(t_far[:h], "y", 1)
    from_next = shift(t_far[h:], "y", -1)
    gate_give = narrow(after(gg1, t_far))
    gate_got = shift(gate_give, "xl", 1)

    from_prev, from_next = lax.optimization_barrier((from_prev, from_next))
    later = after(grads, from_prev)
    rest = jnp.concatenate([term(later, give[j]).astype(BF) for j in (1, 3)], axis=0)
    own_give = term(after(grads, rest), give[0]).astype(BF)
    rest = shift(rest, "core", 1)
    got = {
        1: rest[:rows].astype(F32),
        3: rest[rows:].astype(F32),
        0: shift(own_give, "core", 1).astype(F32),
    }

    zero = jnp.zeros((h, lanes), F32)
    t_next = term(grads, keep[1]) + got[1]
    t_prev = term(grads, keep[3]) + got[3]
    t_next = (t_next + jnp.concatenate([from_prev.astype(F32), zero], axis=0)).astype(BF)
    t_prev = (t_prev + jnp.concatenate([zero, from_next.astype(F32)], axis=0)).astype(BF)
    got_a = shift(t_next, "y", 1)
    got_b = shift(t_prev, "y", -1)
    up_give = narrow(after(gu1, t_next, t_prev, d_got))
    up_got = shift(up_give, "xl", 1)
    got_a, got_b = lax.optimization_barrier((got_a, got_b))
    t_own = term(after(grads, up_give), keep[0]) + got[0]
    t_own = (t_own + got_a.astype(F32) + got_b.astype(F32)).astype(BF)

    w_own = narrow(after(jnp.concatenate([gg0, gu0], axis=1), got_a, gate_got))
    d_own = down(after(a0, w_own))
    back = lax.all_to_all(
        t_own.reshape(peers, cap, lanes), EX, 0, 0, tiled=True
    ).reshape(rows, lanes)

    part = dot(placing, back[:, : 2 * piece], 0, 0)
    x_own = jnp.where(xl == 0, part[:, :piece], part[:, piece:])
    x_give = jnp.where(xl == 0, part[:, piece:], part[:, :piece])
    grad_tokens = (x_own + shift(x_give.astype(BF), "xl", 1).astype(F32)).astype(BF)

    pair_back = back[:, 2 * piece : 2 * piece + 1].astype(F32)
    of_token = jnp.sum(jnp.where(match, pair_back.reshape(peers, cap, 1), 0.0), axis=1)
    pair_sum = jnp.sum(jnp.where(hit, of_token[:, None, :], 0.0), axis=0)
    pair_sum = total(pair_sum, "xl")
    grad_gates = (pair_sum / gates_t).T

    def paired(own, got):
        return jnp.stack([jnp.where(xl == 0, own, got), jnp.where(xl == 0, got, own)])

    grad_gate = paired(w_own[:, :half], gate_got)
    grad_down = paired(d_own, d_got)
    up_got = after(up_got, x_give, grad_gate, grad_down)
    grad_up = paired(w_own[:, half:], up_got)
    return grad_tokens, grad_gates, grad_gate, grad_up, grad_down


def solution(mesh):
    fine = Mesh(mesh.devices.reshape(4, 2, 2, 8, 2), DP + EX)
    return jax.shard_map(
        per_device,
        mesh=fine,
        in_specs=(
            P(EX, DP),
            P(EX, DP),
            P(EX, None),
            P(EX, None),
            P(EX, None, DP),
            P(EX, None, DP),
            P(EX, DP, None),
        ),
        out_specs=(
            P(EX, DP),
            P(EX, None),
            P(EX, None, DP),
            P(EX, None, DP),
            P(EX, DP, None),
        ),
        check_vma=False,
    )
```
